32 devices in a mesh: ctx: 16 (over z, y, x), chan: 2 (over core).
Axes of the slice: x: 2, y: 2, z: 4, core: 2. Of those that a mesh axis runs over, the one named last changes fastest.
Arguments:
- tokens: bfloat16 [131072, 512], P('ctx', 'chan'), parts along dimension 1, may hold values from -6 to 6
- conv_taps: float32 [3, 512], P(None, 'chan'), parts along dimension 1, may hold values from -3 to 3
- gate_weight: bfloat16 [512, 256], P('chan'), parts along dimension 0, may hold values from -0.375 to 0.375
- row_factor: bfloat16 [256, 512, 512], P('ctx'), may hold values from -1 to 2
- col_factor: bfloat16 [512, 256, 256], P('ctx'), may hold values from -1 to 2
- cotangent: bfloat16 [512, 256, 512], P('ctx', None, 'chan'), parts along dimension 2, may hold values from -0.0390625 to 0.0390625
Outputs:
- mixed: bfloat16 [512, 256, 512], P('ctx', None, 'chan'), parts along dimension 2
- conv_grad: float32 [3, 512], P(None, 'chan'), parts along dimension 1
- gate_grad: float32 [512, 256], P('chan'), parts along dimension 0
The draws below stay inside these ranges and needn't reach their ends.
There are 2 independent parts, one for each index of `chan`. The reference program is written for one: setup_inputs(seed, part) draws one part's arguments, and reference() takes and returns one part's arrays. A program takes and returns all parts, laid end to end along the dimension named above; an argument that names none is the same for every part. Nothing has to cross between parts.
All inputs are finite; a program needn't handle non-finite values.
Results may differ from the reference program's by a relative error of at most 0.0057.
Values may be sent and summed in bfloat16 or wider, within the bound.
No kernel may reach another device: no remote copies, remote signals or barrier semaphores. Data moves between devices by JAX's collectives and lax.ppermute only.
A program may use at most 128 MiB of HBM per device.

```python
import jax
import jax.numpy as jnp

BLK = 512
NB = 256
CH = 256
TOKENS = 131072


def dominant_blocks(key, count, order):
    noise = jnp.clip(jax.random.normal(key, (count, order, order), jnp.float32), -4.0, 4.0)
    ident = jnp.eye(order, dtype=jnp.float32)
    return (noise * (0.5 / order ** 0.5) + ident[None]).astype(jnp.bfloat16)


def draw_row_factor(key, part):
    return dominant_blocks(jax.random.fold_in(key, 11), NB, BLK)


def draw_col_factor(key, part):
    return dominant_blocks(jax.random.fold_in(key, 23), BLK, NB)


def level_of(key, dims, cuts, least, high):
    factor_of, own = 1.0, jax.random.fold_in(key, 6)
    for axis_at, blocks in cuts:
        steps = jnp.exp(jax.random.uniform(jax.random.fold_in(own, axis_at), (blocks,), jnp.float32, least / len(cuts), high / len(cuts)))
        factor_of = factor_of * jnp.repeat(steps, dims[axis_at] // blocks).reshape([-1 if axis == axis_at else 1 for axis in range(len(dims))])
    return factor_of


def bell_draw(stream_key, shape, width, limit, split=(), held_as=jnp.bfloat16):
    loudness = level_of(stream_key, shape, split, -0.22, 0.18) if split else 1.0
    values = jax.random.normal(stream_key, shape, jnp.float32) * width * loudness
    return jnp.minimum(jnp.maximum(values, -limit), limit).astype(held_as)


def setup_inputs(seed: int = 0, part: int = 0) -> dict:
    splits = jax.random.split(jax.random.key(seed), 7)
    own_keys = jax.random.split(jax.random.fold_in(splits[6], part), 7)
    return {
        "tokens": bell_draw(own_keys[0], (TOKENS, CH), 1.0, 6.0, ((0, 16),)),
        "conv_taps": bell_draw(own_keys[1], (3, CH), 0.6, 3.0, (), jnp.float32),
        "gate_weight": bell_draw(own_keys[2], (CH, CH), CH ** -0.5, 0.375),
        "row_factor": draw_row_factor(jax.random.fold_in(splits[6], 71), part),
        "col_factor": draw_col_factor(jax.random.fold_in(splits[6], 71), part),
        "cotangent": bell_draw(own_keys[5], (BLK, NB, CH), (TOKENS ** -0.5), 0.0390625, ((0, 16),)),
    }


def reference(tokens, conv_taps, gate_weight, row_factor, col_factor, cotangent):
    padded = jnp.pad(tokens, ((1, 1), (0, 0)))
    conv = conv_taps[0] * padded[0:TOKENS] + conv_taps[1] * padded[1:TOKENS + 1] + conv_taps[2] * padded[2:TOKENS + 2]
    gate = jnp.dot(tokens, gate_weight, preferred_element_type=jnp.float32)
    sig = jax.nn.sigmoid(gate)
    gated = (conv * sig).astype(jnp.bfloat16)
    rows = gated.reshape(NB, BLK, CH).astype(jnp.float32)
    first = jnp.einsum("rdc,rck->rdk", row_factor.astype(jnp.float32), rows).astype(jnp.bfloat16)
    mixed = jnp.einsum("dqr,rdk->dqk", col_factor.astype(jnp.float32), first.astype(jnp.float32)).astype(jnp.bfloat16)
    back_first = jnp.einsum("dqr,dqk->rdk", col_factor.astype(jnp.float32), cotangent.astype(jnp.float32)).astype(jnp.bfloat16)
    back_gated = jnp.einsum("rdc,rdk->rck", row_factor.astype(jnp.float32), back_first.astype(jnp.float32)).reshape(TOKENS, CH)
    back_conv = back_gated * sig
    back_gate = (back_gated * conv * sig * (1.0 - sig)).astype(jnp.bfloat16)
    conv_grad = jnp.stack([jnp.sum(back_conv * padded[j:j + TOKENS].astype(jnp.float32), axis=0) for j in range(3)])
    gate_grad = jnp.dot(tokens.T, back_gate, preferred_element_type=jnp.float32)
    return mixed, conv_grad, gate_grad
```

```python
import functools

import jax
import jax.numpy as jnp
from jax import lax
from jax.experimental import pallas as pl
from jax.experimental.pallas import tpu as pltpu
from jax.sharding import PartitionSpec as P

F32 = jnp.float32
BF16 = jnp.bfloat16
LANES = 128
GROUP = 4
BACK_SHARES = (1,)
FORWARD_SHARES = (1,)
VMEM_LIMIT = 60 * 1024 * 1024


def params():
    return pltpu.CompilerParams(vmem_limit_bytes=VMEM_LIMIT)


def cost(flops, moved):
    return pl.CostEstimate(flops=flops, bytes_accessed=moved, transcendentals=0)


def contract_first(lhs, rhs):
    return lax.dot_general(lhs, rhs, (((0,), (0,)), ((), ())), preferred_element_type=F32)


def back_first_kernel(peers, col_ref, cot_ref, out_ref):
    runs = out_ref.shape[2]
    for i in range(col_ref.shape[0]):
        value = contract_first(col_ref[i], cot_ref[i]).astype(BF16)
        out_ref[:, i] = value.reshape(peers, runs, value.shape[1])


def back_first_part(peers, col, cot, start, count, group):
    _, order, runs_all = col.shape
    width = cot.shape[2]
    runs = runs_all // peers
    base = start // group
    return pl.pallas_call(
        functools.partial(back_first_kernel, peers),
        grid=(count // group,),
        in_specs=[
            pl.BlockSpec((group, order, runs_all), lambda i: (base + i, 0, 0)),
            pl.BlockSpec((group, order, width), lambda i: (base + i, 0, 0)),
        ],
        out_specs=pl.BlockSpec((peers, group, runs, width), lambda i: (0, i, 0, 0)),
        out_shape=jax.ShapeDtypeStruct((peers, count, runs, width), BF16),
        compiler_params=params(),
        cost_estimate=cost(
            2 * count * order * runs_all * width, 2 * count * (order * runs_all + 2 * order * width)
        ),
    )(col, cot)


def mixed_kernel(peers, col_ref, recv_ref, *refs):
    out_ref = refs[-1]
    for i in range(col_ref.shape[0]):
        first = recv_ref[:, i]
        first = first.reshape(first.shape[0] * first.shape[1], first.shape[2])
        out_ref[i] = jnp.dot(col_ref[i], first, preferred_element_type=F32).astype(BF16)


def mixed_part(peers, col, recv, start, group, before):
    offsets, order, runs_all = col.shape
    count, runs, width = recv.shape[1:]
    base = start // group
    in_specs = [
        pl.BlockSpec((group, order, runs_all), lambda i: (base + i, 0, 0)),
        pl.BlockSpec((peers, group, runs, width), lambda i: (0, i, 0, 0)),
    ]
    operands = [col, recv]
    aliases = {}
    if before is not None:
        in_specs.append(pl.BlockSpec(memory_space=pl.ANY))
        operands.append(before)
        aliases = {2: 0}
    return pl.pallas_call(
        functools.partial(mixed_kernel, peers),
        grid=(count // group,),
        in_specs=in_specs,
        out_specs=pl.BlockSpec((group, order, width), lambda i: (base + i, 0, 0)),
        out_shape=jax.ShapeDtypeStruct((offsets, order, width), BF16),
        input_output_aliases=aliases,
        compiler_params=params(),
        cost_estimate=cost(
            2 * count * order * runs_all * width, 2 * count * (order * runs_all + 2 * order * width)
        ),
    )(*operands)


def shifted(tokens, before, after):
    count = tokens.shape[0]
    at = lax.broadcasted_iota(jnp.int32, tokens.shape, 0)
    low = jnp.where(at == 0, before, pltpu.roll(tokens, 1, 0))
    high = jnp.where(at == count - 1, after, pltpu.roll(tokens, count - 1, 0))
    return low, high


def conv_and_sig(tokens_ref, ends_ref, taps_ref, weight_ref):
    raw = tokens_ref[0]
    tokens = raw.astype(F32)
    low, high = shifted(tokens, ends_ref[0, 0:1], ends_ref[0, 1:2])
    conv = taps_ref[0:1] * low + taps_ref[1:2] * tokens + taps_ref[2:3] * high
    sig = jax.nn.sigmoid(jnp.dot(raw, weight_ref[...], preferred_element_type=F32))
    return raw, tokens, low, high, conv, sig


def first_kernel(peers, starts, tokens_ref, ends_ref, taps_ref, weight_ref, row_ref, *refs):
    outs, held = refs[:-1], refs[-1]
    run = pl.program_id(0)
    runs = pl.num_programs(0)
    count = tokens_ref.shape[1]
    n_runs = outs[0].shape[2]
    _, _, _, _, conv, sig = conv_and_sig(tokens_ref, ends_ref, taps_ref, weight_ref)
    gated = (conv * sig).astype(BF16)
    value = jnp.dot(row_ref[0], gated, preferred_element_type=F32)
    for lane in range(held.shape[0]):
        held[lane, pl.ds(run, count, stride=n_runs), :] = value[:, lane * LANES : (lane + 1) * LANES]

    @pl.when(run == runs - 1)
    def _():
        per_peer = count // peers
        for out, start in zip(outs, starts):
            rows = out.shape[1] * n_runs
            for peer in range(peers):
                at = (peer * per_peer + start) * n_runs
                for lane in range(held.shape[0]):
                    value = held[lane, pl.ds(at, rows), :].astype(BF16)
                    out[peer, :, :, lane * LANES : (lane + 1) * LANES] = value.reshape(out.shape[1], n_runs, LANES)


def first_parts(peers, tokens, ends, taps, weight, row, counts):
    runs, length, width = tokens.shape
    starts = [sum(counts[:i]) for i in range(len(counts))]
    return pl.pallas_call(
        functools.partial(first_kernel, peers, starts),
        grid=(runs,),
        in_specs=[
            pl.BlockSpec((1, length, width), lambda r: (r, 0, 0)),
            pl.BlockSpec((1, 2, width), lambda r: (r, 0, 0)),
            pl.BlockSpec(taps.shape, lambda r: (0, 0)),
            pl.BlockSpec(weight.shape, lambda r: (0, 0)),
            pl.BlockSpec((1, length, length), lambda r: (r, 0, 0)),
        ],
        out_specs=[pl.BlockSpec((peers, c, runs, width), lambda r: (0, 0, 0, 0)) for c in counts],
        out_shape=[jax.ShapeDtypeStruct((peers, c, runs, width), BF16) for c in counts],
        scratch_shapes=[pltpu.VMEM((width // LANES, length * runs, LANES), F32)],
        compiler_params=params(),
        cost_estimate=cost(
            2 * runs * length * width * (length + width), 2 * runs * length * (length + 2 * width)
        ),
    )(tokens, ends, taps, weight, row)


def gradient_kernel(starts, tokens_ref, ends_ref, taps_ref, weight_ref, row_ref, *refs):
    parts, (gate_ref, taps_grad_ref, held) = refs[:-3], refs[-3:]
    run = pl.program_id(0)
    count = tokens_ref.shape[1]
    peers, _, n_runs, width = parts[0].shape
    per_peer = count // peers

    @pl.when(run == 0)
    def _():
        gate_ref[...] = jnp.zeros_like(gate_ref)
        taps_grad_ref[...] = jnp.zeros_like(taps_grad_ref)
        for part, start in zip(parts, starts):
            rows = part.shape[1] * n_runs
            for peer in range(peers):
                at = (peer * per_peer + start) * n_runs
                for lane in range(held.shape[0]):
                    value = part[peer, :, :, lane * LANES : (lane + 1) * LANES]
                    held[lane, pl.ds(at, rows), :] = value.reshape(rows, LANES).astype(F32)

    raw, tokens, low, high, conv, sig = conv_and_sig(tokens_ref, ends_ref, taps_ref, weight_ref)
    back_first = jnp.concatenate(
        [held[lane, pl.ds(run, count, stride=n_runs), :].astype(BF16) for lane in range(held.shape[0])], axis=1
    )
    back_conv = contract_first(row_ref[0], back_first) * sig
    for j, value in enumerate((low, tokens, high)):
        taps_grad_ref[j : j + 1] += jnp.sum(back_conv * value, axis=0, keepdims=True)
    back_gate = (back_conv * conv * (1.0 - sig)).astype(BF16)
    gate_ref[...] += contract_first(raw, back_gate)


def gradient_share(tokens, ends, taps, weight, row, parts):
    runs, length, width = tokens.shape
    counts = [part.shape[1] for part in parts]
    starts = [sum(counts[:i]) for i in range(len(counts))]
    return pl.pallas_call(
        functools.partial(gradient_kernel, starts),
        grid=(runs,),
        in_specs=[
            pl.BlockSpec((1, length, width), lambda r: (r, 0, 0)),
            pl.BlockSpec((1, 2, width), lambda r: (r, 0, 0)),
            pl.BlockSpec(taps.shape, lambda r: (0, 0)),
            pl.BlockSpec(weight.shape, lambda r: (0, 0)),
            pl.BlockSpec((1, length, length), lambda r: (r, 0, 0)),
        ]
        + [pl.BlockSpec(part.shape, lambda r: (0, 0, 0, 0)) for part in parts],
        out_specs=[
            pl.BlockSpec(weight.shape, lambda r: (0, 0)),
            pl.BlockSpec((8, width), lambda r: (0, 0)),
        ],
        out_shape=[
            jax.ShapeDtypeStruct(weight.shape, F32),
            jax.ShapeDtypeStruct((8, width), F32),
        ],
        scratch_shapes=[pltpu.VMEM((width // LANES, length * runs, LANES), F32)],
        compiler_params=params(),
        cost_estimate=cost(
            2 * runs * length * width * (length + 2 * width),
            2 * runs * length * (length + 2 * width),
        ),
    )(tokens, ends, taps, weight, row, *parts)


def exchange(block):
    return lax.all_to_all(block, "ctx", split_axis=0, concat_axis=0, tiled=True)


def total(value, peers):
    step = 1
    while step < peers:
        value = value + lax.ppermute(value, "ctx", [(i, i ^ step) for i in range(peers)])
        step *= 2
    return value


def shares(count, parts):
    return [count * part // sum(parts) for part in parts]


def local(tokens, conv_taps, gate_weight, row_factor, col_factor, cotangent):
    peers = lax.axis_size("ctx")
    width = tokens.shape[1]
    runs, length, _ = row_factor.shape
    offsets = col_factor.shape[0]
    back_got = []
    start = 0
    for count in shares(offsets, BACK_SHARES):
        block = back_first_part(peers, col_factor, cotangent, start, count, GROUP)
        if back_got:
            block, back_got[-1] = lax.optimization_barrier((block, back_got[-1]))
        back_got.append(exchange(block))
        start += count

    rows = tokens.reshape(runs, length, width)
    up = [(i, i + 1) for i in range(peers - 1)]
    down = [(i + 1, i) for i in range(peers - 1)]
    low = lax.ppermute(rows[-1, -1:], "ctx", up)
    high = lax.ppermute(rows[0, :1], "ctx", down)
    before = jnp.concatenate([low, rows[:-1, -1]], axis=0)
    after = jnp.concatenate([rows[1:, 0], high], axis=0)
    ends = jnp.stack([before, after], axis=1).astype(F32)

    counts = shares(offsets, FORWARD_SHARES)
    sent = first_parts(peers, rows, ends, conv_taps, gate_weight, row_factor, counts)
    sent = list(sent)
    sent[0], back_got[-1] = lax.optimization_barrier((sent[0], back_got[-1]))
    got = [exchange(sent[0])]

    gate_share, taps_share = gradient_share(
        rows, ends, conv_taps, gate_weight, row_factor, back_got
    )
    both = total(jnp.concatenate([gate_share, taps_share], axis=0), peers)

    for block in sent[1:]:
        block, got[-1], both = lax.optimization_barrier((block, got[-1], both))
        got.append(exchange(block))
    n_gate = gate_weight.shape[0]
    gate_grad, conv_grad = both[:n_gate], both[n_gate : n_gate + conv_taps.shape[0]]

    mixed = None
    start = 0
    for block in got:
        mixed = mixed_part(peers, col_factor, block, start, GROUP, mixed)
        start += block.shape[1]
    return (mixed, conv_grad, gate_grad)


def solution(mesh):
    placed = (
        P("ctx", "chan"),
        P(None, "chan"),
        P("chan", None),
        P("ctx", None, None),
        P("ctx", None, None),
        P("ctx", None, "chan"),
    )
    return jax.shard_map(
        local,
        mesh=mesh,
        in_specs=placed,
        out_specs=(P("ctx", None, "chan"), P(None, "chan"), P("chan", None)),
        check_vma=False,
    )
```

```python
import functools

import jax
import jax.numpy as jnp
from jax import lax
from jax.experimental import pallas as pl
from jax.experimental.pallas import tpu as pltpu
from jax.sharding import PartitionSpec as P

F32 = jnp.float32
BF16 = jnp.bfloat16
LANES = 128
GROUP = 4
VMEM_LIMIT = 60 * 1024 * 1024


def params():
    return pltpu.CompilerParams(vmem_limit_bytes=VMEM_LIMIT)


def cost(flops, moved):
    return pl.CostEstimate(flops=flops, bytes_accessed=moved, transcendentals=0)


def contract_first(lhs, rhs):
    return lax.dot_general(lhs, rhs, (((0,), (0,)), ((), ())), preferred_element_type=F32)


def copies(pairs, sems, at):
    return [pltpu.make_async_copy(source, target, sems.at[at + i]) for i, (source, target) in enumerate(pairs)]


def back_first_kernel(peers, group, col, cot, out, col_held, cot_held, out_held, in_sems, out_sems):
    offsets, _, width = cot_held.shape
    runs = out_held.shape[2]
    steps = [pl.ds(start, group) for start in range(0, offsets, group)]
    loads = [
        copies([(col.at[at], col_held.at[at]), (cot.at[at], cot_held.at[at])], in_sems, 2 * i)
        for i, at in enumerate(steps)
    ]
    stores = [copies([(out_held.at[:, at], out.at[:, at])], out_sems, i) for i, at in enumerate(steps)]
    for load in loads:
        for copy in load:
            copy.start()
    for i, at in enumerate(steps):
        for copy in loads[i]:
            copy.wait()
        for d in range(i * group, (i + 1) * group):
            value = contract_first(col_held[d], cot_held[d]).astype(BF16)
            out_held[:, d] = value.reshape(peers, runs, width)
        stores[i][0].start()
    for store in stores:
        store[0].wait()


def back_first_all(peers, col, cot):
    offsets, order, runs_all = col.shape
    width = cot.shape[2]
    shape = (peers, offsets, runs_all // peers, width)
    steps = offsets // GROUP
    return pl.pallas_call(
        functools.partial(back_first_kernel, peers, GROUP),
        in_specs=[pl.BlockSpec(memory_space=pl.ANY)] * 2,
        out_specs=pl.BlockSpec(memory_space=pl.ANY),
        out_shape=jax.ShapeDtypeStruct(shape, BF16),
        scratch_shapes=[
            pltpu.VMEM(col.shape, BF16),
            pltpu.VMEM(cot.shape, BF16),
            pltpu.VMEM(shape, BF16),
            pltpu.SemaphoreType.DMA((2 * steps,)),
            pltpu.SemaphoreType.DMA((steps,)),
        ],
        compiler_params=params(),
        cost_estimate=cost(
            2 * offsets * order * runs_all * width, 2 * offsets * (order * runs_all + 2 * order * width)
        ),
    )(col, cot)


def mixed_kernel(group, col, recv, out, col_held, recv_held, out_held, in_sems, out_sems):
    peers, offsets, runs, width = recv_held.shape
    steps = [pl.ds(start, group) for start in range(0, offsets, group)]
    loads = [
        copies([(col.at[at], col_held.at[at]), (recv.at[:, at], recv_held.at[:, at])], in_sems, 2 * i)
        for i, at in enumerate(steps)
    ]
    stores = [copies([(out_held.at[at], out.at[at])], out_sems, i) for i, at in enumerate(steps)]
    for load in loads:
        for copy in load:
            copy.start()
    for i, at in enumerate(steps):
        for copy in loads[i]:
            copy.wait()
        for d in range(i * group, (i + 1) * group):
            first = recv_held[:, d].reshape(peers * runs, width)
            out_held[d] = jnp.dot(col_held[d], first, preferred_element_type=F32).astype(BF16)
        stores[i][0].start()
    for store in stores:
        store[0].wait()


def mixed_all(col, recv):
    offsets, order, runs_all = col.shape
    width = recv.shape[3]
    shape = (offsets, order, width)
    steps = offsets // GROUP
    return pl.pallas_call(
        functools.partial(mixed_kernel, GROUP),
        in_specs=[pl.BlockSpec(memory_space=pl.ANY)] * 2,
        out_specs=pl.BlockSpec(memory_space=pl.ANY),
        out_shape=jax.ShapeDtypeStruct(shape, BF16),
        scratch_shapes=[
            pltpu.VMEM(col.shape, BF16),
            pltpu.VMEM(recv.shape, BF16),
            pltpu.VMEM(shape, BF16),
            pltpu.SemaphoreType.DMA((2 * steps,)),
            pltpu.SemaphoreType.DMA((steps,)),
        ],
        compiler_params=params(),
        cost_estimate=cost(
            2 * offsets * order * runs_all * width, 2 * offsets * (order * runs_all + 2 * order * width)
        ),
    )(col, recv)


def shifted(tokens, before, after):
    count = tokens.shape[0]
    at = lax.broadcasted_iota(jnp.int32, tokens.shape, 0)
    low = jnp.where(at == 0, before, pltpu.roll(tokens, 1, 0))
    high = jnp.where(at == count - 1, after, pltpu.roll(tokens, count - 1, 0))
    return low, high


def conv_and_sig(tokens_ref, ends_ref, taps_ref, weight_ref):
    raw = tokens_ref[0]
    tokens = raw.astype(F32)
    low, high = shifted(tokens, ends_ref[0, 0:1], ends_ref[0, 1:2])
    conv = taps_ref[0:1] * low + taps_ref[1:2] * tokens + taps_ref[2:3] * high
    sig = jax.nn.sigmoid(jnp.dot(raw, weight_ref[...], preferred_element_type=F32))
    return raw, tokens, low, high, conv, sig


def first_kernel(peers, starts, tokens_ref, ends_ref, taps_ref, weight_ref, row_ref, *refs):
    outs, held = refs[:-1], refs[-1]
    run = pl.program_id(0)
    runs = pl.num_programs(0)
    count = tokens_ref.shape[1]
    n_runs = outs[0].shape[2]
    _, _, _, _, conv, sig = conv_and_sig(tokens_ref, ends_ref, taps_ref, weight_ref)
    gated = (conv * sig).astype(BF16)
    value = jnp.dot(row_ref[0], gated, preferred_element_type=F32)
    for lane in range(held.shape[0]):
        held[lane, pl.ds(run, count, stride=n_runs), :] = value[:, lane * LANES : (lane + 1) * LANES]

    @pl.when(run == runs - 1)
    def _():
        per_peer = count // peers
        for out, start in zip(outs, starts):
            rows = out.shape[1] * n_runs
            for peer in range(peers):
                at = (peer * per_peer + start) * n_runs
                for lane in range(held.shape[0]):
                    value = held[lane, pl.ds(at, rows), :].astype(BF16)
                    out[peer, :, :, lane * LANES : (lane + 1) * LANES] = value.reshape(out.shape[1], n_runs, LANES)


def first_parts(peers, tokens, ends, taps, weight, row, counts):
    runs, length, width = tokens.shape
    starts = [sum(counts[:i]) for i in range(len(counts))]
    return pl.pallas_call(
        functools.partial(first_kernel, peers, starts),
        grid=(runs,),
        in_specs=[
            pl.BlockSpec((1, length, width), lambda r: (r, 0, 0)),
            pl.BlockSpec((1, 2, width), lambda r: (r, 0, 0)),
            pl.BlockSpec(taps.shape, lambda r: (0, 0)),
            pl.BlockSpec(weight.shape, lambda r: (0, 0)),
            pl.BlockSpec((1, length, length), lambda r: (r, 0, 0)),
        ],
        out_specs=[pl.BlockSpec((peers, c, runs, width), lambda r: (0, 0, 0, 0)) for c in counts],
        out_shape=[jax.ShapeDtypeStruct((peers, c, runs, width), BF16) for c in counts],
        scratch_shapes=[pltpu.VMEM((width // LANES, length * runs, LANES), F32)],
        compiler_params=params(),
        cost_estimate=cost(
            2 * runs * length * width * (length + width), 2 * runs * length * (length + 2 * width)
        ),
    )(tokens, ends, taps, weight, row)


def gradient_kernel(starts, tokens_ref, ends_ref, taps_ref, weight_ref, row_ref, *refs):
    parts, (gate_ref, taps_grad_ref, held) = refs[:-3], refs[-3:]
    run = pl.program_id(0)
    count = tokens_ref.shape[1]
    peers, _, n_runs, width = parts[0].shape
    per_peer = count // peers

    @pl.when(run == 0)
    def _():
        gate_ref[...] = jnp.zeros_like(gate_ref)
        taps_grad_ref[...] = jnp.zeros_like(taps_grad_ref)
        for part, start in zip(parts, starts):
            rows = part.shape[1] * n_runs
            for peer in range(peers):
                at = (peer * per_peer + start) * n_runs
                for lane in range(held.shape[0]):
                    value = part[peer, :, :, lane * LANES : (lane + 1) * LANES]
                    held[lane, pl.ds(at, rows), :] = value.reshape(rows, LANES).astype(F32)

    raw, tokens, low, high, conv, sig = conv_and_sig(tokens_ref, ends_ref, taps_ref, weight_ref)
    back_first = jnp.concatenate(
        [held[lane, pl.ds(run, count, stride=n_runs), :].astype(BF16) for lane in range(held.shape[0])], axis=1
    )
    back_conv = contract_first(row_ref[0], back_first) * sig
    for j, value in enumerate((low, tokens, high)):
        taps_grad_ref[j : j + 1] += jnp.sum(back_conv * value, axis=0, keepdims=True)
    back_gate = (back_conv * conv * (1.0 - sig)).astype(BF16)
    gate_ref[...] += contract_first(raw, back_gate)


def gradient_share(tokens, ends, taps, weight, row, parts):
    runs, length, width = tokens.shape
    counts = [part.shape[1] for part in parts]
    starts = [sum(counts[:i]) for i in range(len(counts))]
    return pl.pallas_call(
        functools.partial(gradient_kernel, starts),
        grid=(runs,),
        in_specs=[
            pl.BlockSpec((1, length, width), lambda r: (r, 0, 0)),
            pl.BlockSpec((1, 2, width), lambda r: (r, 0, 0)),
            pl.BlockSpec(taps.shape, lambda r: (0, 0)),
            pl.BlockSpec(weight.shape, lambda r: (0, 0)),
            pl.BlockSpec((1, length, length), lambda r: (r, 0, 0)),
        ]
        + [pl.BlockSpec(part.shape, lambda r: (0, 0, 0, 0)) for part in parts],
        out_specs=[
            pl.BlockSpec(weight.shape, lambda r: (0, 0)),
            pl.BlockSpec((8, width), lambda r: (0, 0)),
        ],
        out_shape=[
            jax.ShapeDtypeStruct(weight.shape, F32),
            jax.ShapeDtypeStruct((8, width), F32),
        ],
        scratch_shapes=[pltpu.VMEM((width // LANES, length * runs, LANES), F32)],
        compiler_params=params(),
        cost_estimate=cost(
            2 * runs * length * width * (length + 2 * width),
            2 * runs * length * (length + 2 * width),
        ),
    )(tokens, ends, taps, weight, row, *parts)


def exchange(block):
    return lax.all_to_all(block, "ctx", split_axis=0, concat_axis=0, tiled=True)


def total(value, peers):
    step = 1
    while step < peers:
        value = value + lax.ppermute(value, "ctx", [(i, i ^ step) for i in range(peers)])
        step *= 2
    return value


def local(tokens, conv_taps, gate_weight, row_factor, col_factor, cotangent):
    peers = lax.axis_size("ctx")
    width = tokens.shape[1]
    runs, length, _ = row_factor.shape
    offsets = col_factor.shape[0]
    rows = tokens.reshape(runs, length, width)
    up = [(i, i + 1) for i in range(peers - 1)]
    down = [(i + 1, i) for i in range(peers - 1)]
    low = lax.ppermute(tokens[-1:], "ctx", up)
    high = lax.ppermute(tokens[:1], "ctx", down)

    block = back_first_all(peers, col_factor, cotangent)
    block, low, high = lax.optimization_barrier((block, low, high))
    back_got = exchange(block)

    before = jnp.concatenate([low, rows[:-1, -1]], axis=0)
    after = jnp.concatenate([rows[1:, 0], high], axis=0)
    ends = jnp.stack([before, after], axis=1).astype(F32)
    (sent,) = first_parts(peers, rows, ends, conv_taps, gate_weight, row_factor, (offsets,))
    sent, back_got = lax.optimization_barrier((sent, back_got))
    got = exchange(sent)

    gate_share, taps_share = gradient_share(
        rows, ends, conv_taps, gate_weight, row_factor, [back_got]
    )
    both = total(jnp.concatenate([gate_share, taps_share], axis=0), peers)
    n_gate = gate_weight.shape[0]
    gate_grad, conv_grad = both[:n_gate], both[n_gate : n_gate + conv_taps.shape[0]]
    return (mixed_all(col_factor, got), conv_grad, gate_grad)


def solution(mesh):
    placed = (
        P("ctx", "chan"),
        P(None, "chan"),
        P("chan", None),
        P("ctx", None, None),
        P("ctx", None, None),
        P("ctx", None, "chan"),
    )
    return jax.shard_map(
        local,
        mesh=mesh,
        in_specs=placed,
        out_specs=(P("ctx", None, "chan"), P(None, "chan"), P("chan", None)),
        check_vma=False,
    )
```

```python
import functools

import jax
import jax.numpy as jnp
from jax import lax
from jax.experimental import pallas as pl
from jax.experimental.pallas import tpu as pltpu
from jax.sharding import PartitionSpec as P

F32 = jnp.float32
BF16 = jnp.bfloat16
LANES = 128
GROUP = 4
QUARTERS = 4
PAD = 8
BACK_PARTS = (1, 3)
FORWARD_PARTS = (3, 1)
VMEM_LIMIT = 60 * 1024 * 1024


def params():
    return pltpu.CompilerParams(vmem_limit_bytes=VMEM_LIMIT)


def cost(flops, moved):
    return pl.CostEstimate(flops=flops, bytes_accessed=moved, transcendentals=0)


def contract_first(lhs, rhs):
    return lax.dot_general(lhs, rhs, (((0,), (0,)), ((), ())), preferred_element_type=F32)


def copies(pairs, sems, at):
    return [pltpu.make_async_copy(source, target, sems.at[at + i]) for i, (source, target) in enumerate(pairs)]


def back_first_kernel(peers, group, first, col, cot, out, col_held, cot_held, out_held, in_sems, out_sems):
    offsets, _, width = cot_held.shape
    runs = out_held.shape[2]
    steps = [pl.ds(start, group) for start in range(0, offsets, group)]
    loads = [
        copies(
            [
                (col.at[pl.ds(first + i * group, group)], col_held.at[at]),
                (cot.at[pl.ds(first + i * group, group)], cot_held.at[at]),
            ],
            in_sems,
            2 * i,
        )
        for i, at in enumerate(steps)
    ]
    stores = [copies([(out_held.at[:, at], out.at[:, at])], out_sems, i) for i, at in enumerate(steps)]
    for load in loads:
        for copy in load:
            copy.start()
    for i, at in enumerate(steps):
        for copy in loads[i]:
            copy.wait()
        for d in range(i * group, (i + 1) * group):
            value = contract_first(col_held[d], cot_held[d]).astype(BF16)
            out_held[:, d] = value.reshape(peers, runs, width)
        stores[i][0].start()
    for store in stores:
        store[0].wait()


def back_first_part(peers, col, cot, start, count):
    _, order, runs_all = col.shape
    width = cot.shape[2]
    shape = (peers, count, runs_all // peers, width)
    steps = count // GROUP
    return pl.pallas_call(
        functools.partial(back_first_kernel, peers, GROUP, start),
        in_specs=[pl.BlockSpec(memory_space=pl.ANY)] * 2,
        out_specs=pl.BlockSpec(memory_space=pl.ANY),
        out_shape=jax.ShapeDtypeStruct(shape, BF16),
        scratch_shapes=[
            pltpu.VMEM((count, order, runs_all), BF16),
            pltpu.VMEM((count, order, width), BF16),
            pltpu.VMEM(shape, BF16),
            pltpu.SemaphoreType.DMA((2 * steps,)),
            pltpu.SemaphoreType.DMA((steps,)),
        ],
        compiler_params=params(),
        cost_estimate=cost(
            2 * count * order * runs_all * width, 2 * count * (order * runs_all + 2 * order * width)
        ),
    )(col, cot)


def mixed_kernel(group, first, col, recv, *refs):
    out, col_held, recv_held, out_held, in_sems, out_sems = refs[-6:]
    peers, offsets, runs, width = recv_held.shape
    steps = [pl.ds(start, group) for start in range(0, offsets, group)]
    rows = [pl.ds(first + start, group) for start in range(0, offsets, group)]
    loads = [
        copies([(col.at[row], col_held.at[at]), (recv.at[:, at], recv_held.at[:, at])], in_sems, 2 * i)
        for i, (row, at) in enumerate(zip(rows, steps))
    ]
    stores = [
        copies([(out_held.at[at], out.at[row])], out_sems, i) for i, (row, at) in enumerate(zip(rows, steps))
    ]
    for load in loads:
        for copy in load:
            copy.start()
    for i in range(len(steps)):
        for copy in loads[i]:
            copy.wait()
        for d in range(i * group, (i + 1) * group):
            value = recv_held[:, d].reshape(peers * runs, width)
            out_held[d] = jnp.dot(col_held[d], value, preferred_element_type=F32).astype(BF16)
        stores[i][0].start()
    for store in stores:
        store[0].wait()


def mixed_part(col, recv, start, before):
    offsets, order, runs_all = col.shape
    count, width = recv.shape[1], recv.shape[3]
    steps = count // GROUP
    operands = [col, recv] if before is None else [col, recv, before]
    return pl.pallas_call(
        functools.partial(mixed_kernel, GROUP, start),
        in_specs=[pl.BlockSpec(memory_space=pl.ANY)] * len(operands),
        out_specs=pl.BlockSpec(memory_space=pl.ANY),
        out_shape=jax.ShapeDtypeStruct((offsets, order, width), BF16),
        input_output_aliases={} if before is None else {2: 0},
        scratch_shapes=[
            pltpu.VMEM((count, order, runs_all), BF16),
            pltpu.VMEM(recv.shape, BF16),
            pltpu.VMEM((count, order, width), BF16),
            pltpu.SemaphoreType.DMA((2 * steps,)),
            pltpu.SemaphoreType.DMA((steps,)),
        ],
        compiler_params=params(),
        cost_estimate=cost(
            2 * count * order * runs_all * width, 2 * count * (order * runs_all + 2 * order * width)
        ),
    )(*operands)


def shifted(tokens, before, after):
    count = tokens.shape[0]
    at = lax.broadcasted_iota(jnp.int32, tokens.shape, 0)
    low = jnp.where(at == 0, before, pltpu.roll(tokens, 1, 0))
    high = jnp.where(at == count - 1, after, pltpu.roll(tokens, count - 1, 0))
    return low, high


def conv_and_sig(tokens_ref, ends_ref, taps_ref, weight_ref):
    raw = tokens_ref[0]
    tokens = raw.astype(F32)
    low, high = shifted(tokens, ends_ref[0, 0:1], ends_ref[0, 1:2])
    conv = taps_ref[0:1] * low + taps_ref[1:2] * tokens + taps_ref[2:3] * high
    sig = jax.nn.sigmoid(jnp.dot(raw, weight_ref[...], preferred_element_type=F32))
    return raw, tokens, low, high, conv, sig


def first_kernel(peers, starts, tokens_ref, ends_ref, taps_ref, weight_ref, row_ref, *refs):
    outs, held = refs[:-1], refs[-1]
    run = pl.program_id(0)
    runs = pl.num_programs(0)
    count = tokens_ref.shape[1]
    n_runs = outs[0].shape[2]
    _, _, _, _, conv, sig = conv_and_sig(tokens_ref, ends_ref, taps_ref, weight_ref)
    gated = (conv * sig).astype(BF16)
    value = jnp.dot(row_ref[0], gated, preferred_element_type=F32)
    for lane in range(held.shape[0]):
        held[lane, pl.ds(run, count, stride=n_runs), :] = value[:, lane * LANES : (lane + 1) * LANES]

    @pl.when(run == runs - 1)
    def _():
        per_peer = count // peers
        for out, start in zip(outs, starts):
            rows = out.shape[1] * n_runs
            for peer in range(peers):
                at = (peer * per_peer + start) * n_runs
                for lane in range(held.shape[0]):
                    value = held[lane, pl.ds(at, rows), :].astype(BF16)
                    out[peer, :, :, lane * LANES : (lane + 1) * LANES] = value.reshape(out.shape[1], n_runs, LANES)


def first_parts(peers, tokens, ends, taps, weight, row, counts):
    runs, length, width = tokens.shape
    starts = [sum(counts[:i]) for i in range(len(counts))]
    return pl.pallas_call(
        functools.partial(first_kernel, peers, starts),
        grid=(runs,),
        in_specs=[
            pl.BlockSpec((1, length, width), lambda r: (r, 0, 0)),
            pl.BlockSpec((1, 2, width), lambda r: (r, 0, 0)),
            pl.BlockSpec(taps.shape, lambda r: (0, 0)),
            pl.BlockSpec(weight.shape, lambda r: (0, 0)),
            pl.BlockSpec((1, length, length), lambda r: (r, 0, 0)),
        ],
        out_specs=[pl.BlockSpec((peers, c, runs, width), lambda r: (0, 0, 0, 0)) for c in counts],
        out_shape=[jax.ShapeDtypeStruct((peers, c, runs, width), BF16) for c in counts],
        scratch_shapes=[pltpu.VMEM((width // LANES, length * runs, LANES), F32)],
        compiler_params=params(),
        cost_estimate=cost(
            2 * runs * length * width * (length + width), 2 * runs * length * (length + 2 * width)
        ),
    )(tokens, ends, taps, weight, row)


def gradient_kernel(starts, tokens_ref, ends_ref, taps_ref, weight_ref, row_ref, *refs):
    parts, (share_ref, held) = refs[:-2], refs[-2:]
    run = pl.program_id(0)
    count = tokens_ref.shape[1]
    peers, _, n_runs, width = parts[0].shape
    per_peer = count // peers
    rows = share_ref.shape[1] - PAD

    @pl.when(run == 0)
    def _():
        share_ref[...] = jnp.zeros_like(share_ref)
        for part, start in zip(parts, starts):
            got = part.shape[1] * n_runs
            for peer in range(peers):
                at = (peer * per_peer + start) * n_runs
                for lane in range(held.shape[0]):
                    value = part[peer, :, :, lane * LANES : (lane + 1) * LANES]
                    held[lane, pl.ds(at, got), :] = value.reshape(got, LANES).astype(F32)

    raw, tokens, low, high, conv, sig = conv_and_sig(tokens_ref, ends_ref, taps_ref, weight_ref)
    back_first = jnp.concatenate(
        [held[lane, pl.ds(run, count, stride=n_runs), :].astype(BF16) for lane in range(held.shape[0])], axis=1
    )
    back_conv = contract_first(row_ref[0], back_first) * sig
    for j, value in enumerate((low, tokens, high)):
        share_ref[j, rows : rows + 1] += jnp.sum(back_conv * value, axis=0, keepdims=True)
    back_gate = (back_conv * conv * (1.0 - sig)).astype(BF16)
    share_ref[:, :rows] += contract_first(raw, back_gate).reshape(QUARTERS, rows, width)


def gradient_share(tokens, ends, taps, weight, row, parts):
    runs, length, width = tokens.shape
    shape = (QUARTERS, weight.shape[0] // QUARTERS + PAD, width)
    counts = [part.shape[1] for part in parts]
    starts = [sum(counts[:i]) for i in range(len(counts))]
    return pl.pallas_call(
        functools.partial(gradient_kernel, starts),
        grid=(runs,),
        in_specs=[
            pl.BlockSpec((1, length, width), lambda r: (r, 0, 0)),
            pl.BlockSpec((1, 2, width), lambda r: (r, 0, 0)),
            pl.BlockSpec(taps.shape, lambda r: (0, 0)),
            pl.BlockSpec(weight.shape, lambda r: (0, 0)),
            pl.BlockSpec((1, length, length), lambda r: (r, 0, 0)),
        ]
        + [pl.BlockSpec(part.shape, lambda r: (0, 0, 0, 0)) for part in parts],
        out_specs=pl.BlockSpec(shape, lambda r: (0, 0, 0)),
        out_shape=jax.ShapeDtypeStruct(shape, F32),
        scratch_shapes=[pltpu.VMEM((width // LANES, length * runs, LANES), F32)],
        compiler_params=params(),
        cost_estimate=cost(
            2 * runs * length * width * (length + 2 * width),
            2 * runs * length * (length + 2 * width),
        ),
    )(tokens, ends, taps, weight, row, *parts)


def exchange(block):
    return lax.all_to_all(block, "ctx", split_axis=0, concat_axis=0, tiled=True)


def swapped(value, step, peers):
    return lax.ppermute(value, "ctx", [(i, i ^ step) for i in range(peers)])


def summed_quarter(share, peers):
    own = lax.axis_index("ctx") % QUARTERS
    quarter = lax.dynamic_index_in_dim(share, own, 0, keepdims=False)
    for step in range(1, QUARTERS):
        other = lax.dynamic_index_in_dim(share, own ^ step, 0, keepdims=False)
        quarter = quarter + swapped(other, step, peers)
    step = QUARTERS
    while step < peers:
        quarter = quarter + swapped(quarter, step, peers)
        step *= 2
    return quarter


def gathered(quarter, peers):
    own = lax.axis_index("ctx") % QUARTERS
    held = [quarter] + [swapped(quarter, step, peers) for step in range(1, QUARTERS)]
    for bit in (1, 2):
        odd = (own & bit) != 0
        held = [jnp.where(odd, held[i ^ bit], held[i]) for i in range(QUARTERS)]
    return held


def split(count, parts):
    return [count * part // sum(parts) for part in parts]


def local(tokens, conv_taps, gate_weight, row_factor, col_factor, cotangent):
    peers = lax.axis_size("ctx")
    width = tokens.shape[1]
    runs, length, _ = row_factor.shape
    offsets = col_factor.shape[0]
    rows = tokens.reshape(runs, length, width)

    back_got = []
    start = 0
    for count in split(offsets, BACK_PARTS):
        block = back_first_part(peers, col_factor, cotangent, start, count)
        if back_got:
            up = [(i, i + 1) for i in range(peers - 1)]
            down = [(i + 1, i) for i in range(peers - 1)]
            low = lax.ppermute(tokens[-1:], "ctx", up)
            high = lax.ppermute(tokens[:1], "ctx", down)
            block, low, high, back_got[0] = lax.optimization_barrier((block, low, high, back_got[0]))
        back_got.append(exchange(block))
        start += count

    before = jnp.concatenate([low, rows[:-1, -1]], axis=0)
    after = jnp.concatenate([rows[1:, 0], high], axis=0)
    ends = jnp.stack([before, after], axis=1).astype(F32)
    counts = split(offsets, FORWARD_PARTS)
    sent = list(first_parts(peers, rows, ends, conv_taps, gate_weight, row_factor, counts))
    sent[0], back_got[-1] = lax.optimization_barrier((sent[0], back_got[-1]))
    got = [exchange(sent[0])]

    share = gradient_share(rows, ends, conv_taps, gate_weight, row_factor, back_got)
    quarter = summed_quarter(share, peers)
    sent[1], got[0], quarter = lax.optimization_barrier((sent[1], got[0], quarter))
    got.append(exchange(sent[1]))
    held = gathered(quarter, peers)
    n_rows = quarter.shape[0] - PAD
    gate_grad = jnp.concatenate([part[:n_rows] for part in held], axis=0)
    conv_grad = jnp.concatenate([part[n_rows : n_rows + 1] for part in held[: conv_taps.shape[0]]], axis=0)

    mixed = mixed_part(col_factor, got[0], 0, None)
    mixed = mixed_part(col_factor, got[1], counts[0], mixed)
    return (mixed, conv_grad, gate_grad)


def solution(mesh):
    placed = (
        P("ctx", "chan"),
        P(None, "chan"),
        P("chan", None),
        P("ctx", None, None),
        P("ctx", None, None),
        P("ctx", None, "chan"),
    )
    return jax.shard_map(
        local,
        mesh=mesh,
        in_specs=placed,
        out_specs=(P("ctx", None, "chan"), P(None, "chan"), P("chan", None)),
        check_vma=False,
    )
```

```python
import functools

import jax
import jax.numpy as jnp
from jax import lax
from jax.experimental import pallas as pl
from jax.experimental.pallas import tpu as pltpu
from jax.sharding import PartitionSpec as P

F32 = jnp.float32
BF16 = jnp.bfloat16
LANES = 128
GROUP = 4
QUARTERS = 4
PAD = 8
BACK_PARTS = (1, 3)
FORWARD_PARTS = (3, 1)
VMEM_LIMIT = 63 * 1024 * 1024 + 768 * 1024


def params():
    return pltpu.CompilerParams(vmem_limit_bytes=VMEM_LIMIT)


def cost(flops, moved):
    return pl.CostEstimate(flops=flops, bytes_accessed=moved, transcendentals=0)


def contract_first(lhs, rhs):
    return lax.dot_general(lhs, rhs, (((0,), (0,)), ((), ())), preferred_element_type=F32)


def copies(pairs, sems, at):
    return [pltpu.make_async_copy(source, target, sems.at[at + i]) for i, (source, target) in enumerate(pairs)]


def back_first_kernel(peers, group, first, col, cot, out, col_held, cot_held, out_held, in_sems, out_sems):
    offsets, _, width = cot_held.shape
    runs = out_held.shape[2]
    steps = [pl.ds(start, group) for start in range(0, offsets, group)]
    loads = [
        copies(
            [
                (col.at[pl.ds(first + i * group, group)], col_held.at[at]),
                (cot.at[pl.ds(first + i * group, group)], cot_held.at[at]),
            ],
            in_sems,
            2 * i,
        )
        for i, at in enumerate(steps)
    ]
    stores = [copies([(out_held.at[:, at], out.at[:, at])], out_sems, i) for i, at in enumerate(steps)]
    for load in loads:
        for copy in load:
            copy.start()
    for i, at in enumerate(steps):
        for copy in loads[i]:
            copy.wait()
        for d in range(i * group, (i + 1) * group):
            value = contract_first(col_held[d], cot_held[d]).astype(BF16)
            out_held[:, d] = value.reshape(peers, runs, width)
        stores[i][0].start()
    for store in stores:
        store[0].wait()


def back_first_part(peers, col, cot, start, count):
    _, order, runs_all = col.shape
    width = cot.shape[2]
    shape = (peers, count, runs_all // peers, width)
    steps = count // GROUP
    return pl.pallas_call(
        functools.partial(back_first_kernel, peers, GROUP, start),
        in_specs=[pl.BlockSpec(memory_space=pl.ANY)] * 2,
        out_specs=pl.BlockSpec(memory_space=pl.ANY),
        out_shape=jax.ShapeDtypeStruct(shape, BF16),
        scratch_shapes=[
            pltpu.VMEM((count, order, runs_all), BF16),
            pltpu.VMEM((count, order, width), BF16),
            pltpu.VMEM(shape, BF16),
            pltpu.SemaphoreType.DMA((2 * steps,)),
            pltpu.SemaphoreType.DMA((steps,)),
        ],
        compiler_params=params(),
        cost_estimate=cost(
            2 * count * order * runs_all * width, 2 * count * (order * runs_all + 2 * order * width)
        ),
    )(col, cot)


def mixed_kernel(group, first, col, recv, *refs):
    out, col_held, recv_held, out_held, in_sems, out_sems = refs[-6:]
    peers, offsets, runs, width = recv_held.shape
    steps = [pl.ds(start, group) for start in range(0, offsets, group)]
    rows = [pl.ds(first + start, group) for start in range(0, offsets, group)]
    loads = [
        copies([(col.at[row], col_held.at[at]), (recv.at[:, at], recv_held.at[:, at])], in_sems, 2 * i)
        for i, (row, at) in enumerate(zip(rows, steps))
    ]
    stores = [
        copies([(out_held.at[at], out.at[row])], out_sems, i) for i, (row, at) in enumerate(zip(rows, steps))
    ]
    for load in loads:
        for copy in load:
            copy.start()
    for i in range(len(steps)):
        for copy in loads[i]:
            copy.wait()
        for d in range(i * group, (i + 1) * group):
            value = recv_held[:, d].reshape(peers * runs, width)
            out_held[d] = jnp.dot(col_held[d], value, preferred_element_type=F32).astype(BF16)
        stores[i][0].start()
    for store in stores:
        store[0].wait()


def mixed_part(col, recv, start, before):
    offsets, order, runs_all = col.shape
    count, width = recv.shape[1], recv.shape[3]
    steps = count // GROUP
    operands = [col, recv] if before is None else [col, recv, before]
    return pl.pallas_call(
        functools.partial(mixed_kernel, GROUP, start),
        in_specs=[pl.BlockSpec(memory_space=pl.ANY)] * len(operands),
        out_specs=pl.BlockSpec(memory_space=pl.ANY),
        out_shape=jax.ShapeDtypeStruct((offsets, order, width), BF16),
        input_output_aliases={} if before is None else {2: 0},
        scratch_shapes=[
            pltpu.VMEM((count, order, runs_all), BF16),
            pltpu.VMEM(recv.shape, BF16),
            pltpu.VMEM((count, order, width), BF16),
            pltpu.SemaphoreType.DMA((2 * steps,)),
            pltpu.SemaphoreType.DMA((steps,)),
        ],
        compiler_params=params(),
        cost_estimate=cost(
            2 * count * order * runs_all * width, 2 * count * (order * runs_all + 2 * order * width)
        ),
    )(*operands)


def shifted(tokens, before, after):
    count = tokens.shape[0]
    at = lax.broadcasted_iota(jnp.int32, tokens.shape, 0)
    low = jnp.where(at == 0, before, pltpu.roll(tokens, 1, 0))
    high = jnp.where(at == count - 1, after, pltpu.roll(tokens, count - 1, 0))
    return low, high


def conv_and_sig(tokens_ref, ends_ref, taps_ref, weight_ref):
    raw = tokens_ref[0]
    tokens = raw.astype(F32)
    low, high = shifted(tokens, ends_ref[0, 0:1], ends_ref[0, 1:2])
    conv = taps_ref[0:1] * low + taps_ref[1:2] * tokens + taps_ref[2:3] * high
    sig = jax.nn.sigmoid(jnp.dot(raw, weight_ref[...], preferred_element_type=F32))
    return raw, tokens, low, high, conv, sig


def first_kernel(peers, starts, tokens_ref, ends_ref, taps_ref, weight_ref, row_ref, *refs):
    outs, held = refs[:-1], refs[-1]
    run = pl.program_id(0)
    runs = pl.num_programs(0)
    count = tokens_ref.shape[1]
    n_runs = outs[0].shape[2]
    _, _, _, _, conv, sig = conv_and_sig(tokens_ref, ends_ref, taps_ref, weight_ref)
    gated = (conv * sig).astype(BF16)
    value = jnp.dot(row_ref[0], gated, preferred_element_type=F32)
    for lane in range(held.shape[0]):
        held[lane, pl.ds(run, count, stride=n_runs), :] = value[:, lane * LANES : (lane + 1) * LANES]

    @pl.when(run == runs - 1)
    def _():
        per_peer = count // peers
        for out, start in zip(outs, starts):
            rows = out.shape[1] * n_runs
            for peer in range(peers):
                at = (peer * per_peer + start) * n_runs
                for lane in range(held.shape[0]):
                    value = held[lane, pl.ds(at, rows), :].astype(BF16)
                    out[peer, :, :, lane * LANES : (lane + 1) * LANES] = value.reshape(out.shape[1], n_runs, LANES)


def first_parts(peers, tokens, ends, taps, weight, row, counts):
    runs, length, width = tokens.shape
    starts = [sum(counts[:i]) for i in range(len(counts))]
    return pl.pallas_call(
        functools.partial(first_kernel, peers, starts),
        grid=(runs,),
        in_specs=[
            pl.BlockSpec((1, length, width), lambda r: (r, 0, 0)),
            pl.BlockSpec((1, 2, width), lambda r: (r, 0, 0)),
            pl.BlockSpec(taps.shape, lambda r: (0, 0)),
            pl.BlockSpec(weight.shape, lambda r: (0, 0)),
            pl.BlockSpec((1, length, length), lambda r: (r, 0, 0)),
        ],
        out_specs=[pl.BlockSpec((peers, c, runs, width), lambda r: (0, 0, 0, 0)) for c in counts],
        out_shape=[jax.ShapeDtypeStruct((peers, c, runs, width), BF16) for c in counts],
        scratch_shapes=[pltpu.VMEM((width // LANES, length * runs, LANES), F32)],
        compiler_params=params(),
        cost_estimate=cost(
            2 * runs * length * width * (length + width), 2 * runs * length * (length + 2 * width)
        ),
    )(tokens, ends, taps, weight, row)


def gradient_kernel(starts, tokens_ref, ends_ref, taps_ref, weight_ref, row_ref, *refs):
    parts, (share_ref, held) = refs[:-2], refs[-2:]
    run = pl.program_id(0)
    count = tokens_ref.shape[1]
    peers, _, n_runs, width = parts[0].shape
    per_peer = count // peers
    rows = share_ref.shape[1] - PAD

    @pl.when(run == 0)
    def _():
        share_ref[...] = jnp.zeros_like(share_ref)
        for part, start in zip(parts, starts):
            got = part.shape[1] * n_runs
            for peer in range(peers):
                at = (peer * per_peer + start) * n_runs
                for lane in range(held.shape[0]):
                    value = part[peer, :, :, lane * LANES : (lane + 1) * LANES]
                    held[lane, pl.ds(at, got), :] = value.reshape(got, LANES).astype(F32)

    raw, tokens, low, high, conv, sig = conv_and_sig(tokens_ref, ends_ref, taps_ref, weight_ref)
    back_first = jnp.concatenate(
        [held[lane, pl.ds(run, count, stride=n_runs), :].astype(BF16) for lane in range(held.shape[0])], axis=1
    )
    back_conv = contract_first(row_ref[0], back_first) * sig
    for j, value in enumerate((low, tokens, high)):
        share_ref[j, rows : rows + 1] += jnp.sum(back_conv * value, axis=0, keepdims=True)
    back_gate = (back_conv * conv * (1.0 - sig)).astype(BF16)
    share_ref[:, :rows] += contract_first(raw, back_gate).reshape(QUARTERS, rows, width)


def gradient_share(tokens, ends, taps, weight, row, parts):
    runs, length, width = tokens.shape
    shape = (QUARTERS, weight.shape[0] // QUARTERS + PAD, width)
    counts = [part.shape[1] for part in parts]
    starts = [sum(counts[:i]) for i in range(len(counts))]
    return pl.pallas_call(
        functools.partial(gradient_kernel, starts),
        grid=(runs,),
        in_specs=[
            pl.BlockSpec((1, length, width), lambda r: (r, 0, 0)),
            pl.BlockSpec((1, 2, width), lambda r: (r, 0, 0)),
            pl.BlockSpec(taps.shape, lambda r: (0, 0)),
            pl.BlockSpec(weight.shape, lambda r: (0, 0)),
            pl.BlockSpec((1, length, length), lambda r: (r, 0, 0)),
        ]
        + [pl.BlockSpec(part.shape, lambda r: (0, 0, 0, 0)) for part in parts],
        out_specs=pl.BlockSpec(shape, lambda r: (0, 0, 0)),
        out_shape=jax.ShapeDtypeStruct(shape, F32),
        scratch_shapes=[pltpu.VMEM((width // LANES, length * runs, LANES), F32)],
        compiler_params=params(),
        cost_estimate=cost(
            2 * runs * length * width * (length + 2 * width),
            2 * runs * length * (length + 2 * width),
        ),
    )(tokens, ends, taps, weight, row, *parts)


def exchange(block):
    return lax.all_to_all(block, "ctx", split_axis=0, concat_axis=0, tiled=True)


def swapped(value, step, peers):
    return lax.ppermute(value, "ctx", [(i, i ^ step) for i in range(peers)])


def summed_quarter(share, peers):
    own = lax.axis_index("ctx") % QUARTERS
    quarter = lax.dynamic_index_in_dim(share, own, 0, keepdims=False)
    for step in range(1, QUARTERS):
        other = lax.dynamic_index_in_dim(share, own ^ step, 0, keepdims=False)
        quarter = quarter + swapped(other, step, peers)
    step = QUARTERS
    while step < peers:
        quarter = quarter + swapped(quarter, step, peers)
        step *= 2
    return quarter


def gathered(quarter, peers):
    own = lax.axis_index("ctx") % QUARTERS
    held = [quarter] + [swapped(quarter, step, peers) for step in range(1, QUARTERS)]
    for bit in (1, 2):
        odd = (own & bit) != 0
        held = [jnp.where(odd, held[i ^ bit], held[i]) for i in range(QUARTERS)]
    return held


def split(count, parts):
    return [count * part // sum(parts) for part in parts]


def local(tokens, conv_taps, gate_weight, row_factor, col_factor, cotangent):
    peers = lax.axis_size("ctx")
    width = tokens.shape[1]
    runs, length, _ = row_factor.shape
    offsets = col_factor.shape[0]
    rows = tokens.reshape(runs, length, width)

    back_got = []
    start = 0
    for count in split(offsets, BACK_PARTS):
        block = back_first_part(peers, col_factor, cotangent, start, count)
        if back_got:
            up = [(i, i + 1) for i in range(peers - 1)]
            down = [(i + 1, i) for i in range(peers - 1)]
            low = lax.ppermute(tokens[-1:], "ctx", up)
            high = lax.ppermute(tokens[:1], "ctx", down)
            block, low, high, back_got[0] = lax.optimization_barrier((block, low, high, back_got[0]))
        back_got.append(exchange(block))
        start += count

    before = jnp.concatenate([low, rows[:-1, -1]], axis=0)
    after = jnp.concatenate([rows[1:, 0], high], axis=0)
    ends = jnp.stack([before, after], axis=1).astype(F32)
    counts = split(offsets, FORWARD_PARTS)
    sent = list(first_parts(peers, rows, ends, conv_taps, gate_weight, row_factor, counts))
    sent[0], back_got[-1] = lax.optimization_barrier((sent[0], back_got[-1]))
    got = [exchange(sent[0])]

    share = gradient_share(rows, ends, conv_taps, gate_weight, row_factor, back_got)
    quarter = summed_quarter(share, peers)
    sent[1], got[0], quarter = lax.optimization_barrier((sent[1], got[0], quarter))
    got.append(exchange(sent[1]))
    held = gathered(quarter, peers)
    n_rows = quarter.shape[0] - PAD
    gate_grad = jnp.concatenate([part[:n_rows] for part in held], axis=0)
    conv_grad = jnp.concatenate([part[n_rows : n_rows + 1] for part in held[: conv_taps.shape[0]]], axis=0)

    mixed = mixed_part(col_factor, got[0], 0, None)
    mixed = mixed_part(col_factor, got[1], counts[0], mixed)
    return (mixed, conv_grad, gate_grad)


def solution(mesh):
    placed = (
        P("ctx", "chan"),
        P(None, "chan"),
        P("chan", None),
        P("ctx", None, None),
        P("ctx", None, None),
        P("ctx", None, "chan"),
    )
    return jax.shard_map(
        local,
        mesh=mesh,
        in_specs=placed,
        out_specs=(P("ctx", None, "chan"), P(None, "chan"), P("chan", None)),
        check_vma=False,
    )
```

```python
import functools

import jax
import jax.numpy as jnp
from jax import lax
from jax.experimental import pallas as pl
from jax.experimental.pallas import tpu as pltpu
from jax.sharding import PartitionSpec as P

F32 = jnp.float32
BF16 = jnp.bfloat16
LANES = 128
GROUP = 4
QUARTERS = 4
PAD = 8
BACK_PARTS = (1, 3)
FORWARD_PARTS = (3, 1)
VMEM_LIMIT = 63 * 1024 * 1024 + 768 * 1024


def params():
    return pltpu.CompilerParams(vmem_limit_bytes=VMEM_LIMIT)


def cost(flops, moved):
    return pl.CostEstimate(flops=flops, bytes_accessed=moved, transcendentals=0)


def contract_first(lhs, rhs):
    return lax.dot_general(lhs, rhs, (((0,), (0,)), ((), ())), preferred_element_type=F32)


def copies(pairs, sems, at):
    return [pltpu.make_async_copy(source, target, sems.at[at + i]) for i, (source, target) in enumerate(pairs)]


def back_first_kernel(peers, group, first, col, cot, out, col_held, cot_held, out_held, in_sems, out_sems):
    offsets, _, width = cot_held.shape
    runs = out_held.shape[2]
    steps = [pl.ds(start, group) for start in range(0, offsets, group)]
    loads = [
        copies(
            [
                (col.at[pl.ds(first + i * group, group)], col_held.at[at]),
                (cot.at[pl.ds(first + i * group, group)], cot_held.at[at]),
            ],
            in_sems,
            2 * i,
        )
        for i, at in enumerate(steps)
    ]
    stores = [copies([(out_held.at[:, at], out.at[:, at])], out_sems, i) for i, at in enumerate(steps)]
    for load in loads:
        for copy in load:
            copy.start()
    for i, at in enumerate(steps):
        for copy in loads[i]:
            copy.wait()
        for d in range(i * group, (i + 1) * group):
            value = contract_first(col_held[d], cot_held[d]).astype(BF16)
            out_held[:, d] = value.reshape(peers, runs, width)
        stores[i][0].start()
    for store in stores:
        store[0].wait()


def back_first_part(peers, col, cot, start, count):
    _, order, runs_all = col.shape
    width = cot.shape[2]
    shape = (peers, count, runs_all // peers, width)
    steps = count // GROUP
    return pl.pallas_call(
        functools.partial(back_first_kernel, peers, GROUP, start),
        in_specs=[pl.BlockSpec(memory_space=pl.ANY)] * 2,
        out_specs=pl.BlockSpec(memory_space=pl.ANY),
        out_shape=jax.ShapeDtypeStruct(shape, BF16),
        scratch_shapes=[
            pltpu.VMEM((count, order, runs_all), BF16),
            pltpu.VMEM((count, order, width), BF16),
            pltpu.VMEM(shape, BF16),
            pltpu.SemaphoreType.DMA((2 * steps,)),
            pltpu.SemaphoreType.DMA((steps,)),
        ],
        compiler_params=params(),
        cost_estimate=cost(
            2 * count * order * runs_all * width, 2 * count * (order * runs_all + 2 * order * width)
        ),
    )(col, cot)


def mixed_kernel(group, first, col, recv, *refs):
    out, col_held, recv_held, out_held, in_sems, out_sems = refs[-6:]
    peers, offsets, runs, width = recv_held.shape
    steps = [pl.ds(start, group) for start in range(0, offsets, group)]
    rows = [pl.ds(first + start, group) for start in range(0, offsets, group)]
    loads = [
        copies([(col.at[row], col_held.at[at]), (recv.at[:, at], recv_held.at[:, at])], in_sems, 2 * i)
        for i, (row, at) in enumerate(zip(rows, steps))
    ]
    stores = [
        copies([(out_held.at[at], out.at[row])], out_sems, i) for i, (row, at) in enumerate(zip(rows, steps))
    ]
    for load in loads:
        for copy in load:
            copy.start()
    for i in range(len(steps)):
        for copy in loads[i]:
            copy.wait()
        for d in range(i * group, (i + 1) * group):
            value = recv_held[:, d].reshape(peers * runs, width)
            out_held[d] = jnp.dot(col_held[d], value, preferred_element_type=F32).astype(BF16)
        stores[i][0].start()
    for store in stores:
        store[0].wait()


def mixed_part(col, recv, start, before, grant):
    offsets, order, runs_all = col.shape
    count, width = recv.shape[1], recv.shape[3]
    steps = count // GROUP
    operands = [col, recv] if before is None else [col, recv, before]
    return pl.pallas_call(
        functools.partial(mixed_kernel, GROUP, start),
        in_specs=[pl.BlockSpec(memory_space=pl.ANY)] * len(operands),
        out_specs=pl.BlockSpec(memory_space=pl.ANY),
        out_shape=jax.ShapeDtypeStruct((offsets, order, width), BF16),
        input_output_aliases={} if before is None else {2: 0},
        scratch_shapes=[
            pltpu.VMEM((count, order, runs_all), BF16),
            pltpu.VMEM(recv.shape, BF16),
            pltpu.VMEM((count, order, width), BF16),
            pltpu.SemaphoreType.DMA((2 * steps,)),
            pltpu.SemaphoreType.DMA((steps,)),
        ],
        compiler_params=pltpu.CompilerParams(vmem_limit_bytes=grant),
        cost_estimate=cost(
            2 * count * order * runs_all * width, 2 * count * (order * runs_all + 2 * order * width)
        ),
    )(*operands)


def last_mixed_kernel(group, first, col, recv, before, out, out_held, sems):
    peers, offsets, runs, width = recv.shape
    stores = []
    for start in range(0, offsets, group):
        for d in range(start, start + group):
            value = recv[:, d].reshape(peers * runs, width)
            out_held[d] = jnp.dot(col[d], value, preferred_element_type=F32).astype(BF16)
        pair = (out_held.at[pl.ds(start, group)], out.at[pl.ds(first + start, group)])
        stores += copies([pair], sems, len(stores))
        stores[-1].start()
    for store in stores:
        store.wait()


def last_mixed_part(col, recv, start, before):
    count, order, runs_all = col.shape
    width = recv.shape[3]
    steps = count // GROUP
    vmem = pl.BlockSpec(memory_space=pltpu.VMEM)
    return pl.pallas_call(
        functools.partial(last_mixed_kernel, GROUP, start),
        in_specs=[vmem, vmem, pl.BlockSpec(memory_space=pl.ANY)],
        out_specs=pl.BlockSpec(memory_space=pl.ANY),
        out_shape=jax.ShapeDtypeStruct(before.shape, BF16),
        input_output_aliases={2: 0},
        scratch_shapes=[pltpu.VMEM((count, order, width), BF16), pltpu.SemaphoreType.DMA((steps,))],
        compiler_params=pltpu.CompilerParams(vmem_limit_bytes=VMEM_LIMIT // 4),
        cost_estimate=cost(
            2 * count * order * runs_all * width, 2 * count * (order * runs_all + 2 * order * width)
        ),
    )(col, recv, before)


def shifted(tokens, before, after):
    count = tokens.shape[0]
    at = lax.broadcasted_iota(jnp.int32, tokens.shape, 0)
    low = jnp.where(at == 0, before, pltpu.roll(tokens, 1, 0))
    high = jnp.where(at == count - 1, after, pltpu.roll(tokens, count - 1, 0))
    return low, high


def conv_and_sig(tokens_ref, ends_ref, taps_ref, weight_ref):
    raw = tokens_ref[0]
    tokens = raw.astype(F32)
    low, high = shifted(tokens, ends_ref[0, 0:1], ends_ref[0, 1:2])
    conv = taps_ref[0:1] * low + taps_ref[1:2] * tokens + taps_ref[2:3] * high
    sig = jax.nn.sigmoid(jnp.dot(raw, weight_ref[...], preferred_element_type=F32))
    return raw, tokens, low, high, conv, sig


def first_kernel(peers, starts, tokens_ref, ends_ref, taps_ref, weight_ref, row_ref, *refs):
    outs, held = refs[:-1], refs[-1]
    run = pl.program_id(0)
    runs = pl.num_programs(0)
    count = tokens_ref.shape[1]
    n_runs = outs[0].shape[2]
    _, _, _, _, conv, sig = conv_and_sig(tokens_ref, ends_ref, taps_ref, weight_ref)
    gated = (conv * sig).astype(BF16)
    value = jnp.dot(row_ref[0], gated, preferred_element_type=F32)
    for lane in range(held.shape[0]):
        held[lane, pl.ds(run, count, stride=n_runs), :] = value[:, lane * LANES : (lane + 1) * LANES]

    @pl.when(run == runs - 1)
    def _():
        per_peer = count // peers
        for out, start in zip(outs, starts):
            rows = out.shape[1] * n_runs
            for peer in range(peers):
                at = (peer * per_peer + start) * n_runs
                for lane in range(held.shape[0]):
                    value = held[lane, pl.ds(at, rows), :].astype(BF16)
                    out[peer, :, :, lane * LANES : (lane + 1) * LANES] = value.reshape(out.shape[1], n_runs, LANES)


def first_parts(peers, tokens, ends, taps, weight, row, counts):
    runs, length, width = tokens.shape
    starts = [sum(counts[:i]) for i in range(len(counts))]
    return pl.pallas_call(
        functools.partial(first_kernel, peers, starts),
        grid=(runs,),
        in_specs=[
            pl.BlockSpec((1, length, width), lambda r: (r, 0, 0)),
            pl.BlockSpec((1, 2, width), lambda r: (r, 0, 0)),
            pl.BlockSpec(taps.shape, lambda r: (0, 0)),
            pl.BlockSpec(weight.shape, lambda r: (0, 0)),
            pl.BlockSpec((1, length, length), lambda r: (r, 0, 0)),
        ],
        out_specs=[pl.BlockSpec((peers, c, runs, width), lambda r: (0, 0, 0, 0)) for c in counts],
        out_shape=[jax.ShapeDtypeStruct((peers, c, runs, width), BF16) for c in counts],
        scratch_shapes=[pltpu.VMEM((width // LANES, length * runs, LANES), F32)],
        compiler_params=params(),
        cost_estimate=cost(
            2 * runs * length * width * (length + width), 2 * runs * length * (length + 2 * width)
        ),
    )(tokens, ends, taps, weight, row)


def gradient_kernel(starts, tokens_ref, ends_ref, taps_ref, weight_ref, row_ref, *refs):
    parts, (share_ref, held) = refs[:-2], refs[-2:]
    run = pl.program_id(0)
    count = tokens_ref.shape[1]
    peers, _, n_runs, width = parts[0].shape
    per_peer = count // peers
    rows = share_ref.shape[1] - PAD

    @pl.when(run == 0)
    def _():
        share_ref[...] = jnp.zeros_like(share_ref)
        for part, start in zip(parts, starts):
            got = part.shape[1] * n_runs
            for peer in range(peers):
                at = (peer * per_peer + start) * n_runs
                for lane in range(held.shape[0]):
                    value = part[peer, :, :, lane * LANES : (lane + 1) * LANES]
                    held[lane, pl.ds(at, got), :] = value.reshape(got, LANES).astype(F32)

    raw, tokens, low, high, conv, sig = conv_and_sig(tokens_ref, ends_ref, taps_ref, weight_ref)
    back_first = jnp.concatenate(
        [held[lane, pl.ds(run, count, stride=n_runs), :].astype(BF16) for lane in range(held.shape[0])], axis=1
    )
    back_conv = contract_first(row_ref[0], back_first) * sig
    for j, value in enumerate((low, tokens, high)):
        share_ref[j, rows : rows + 1] += jnp.sum(back_conv * value, axis=0, keepdims=True)
    back_gate = (back_conv * conv * (1.0 - sig)).astype(BF16)
    share_ref[:, :rows] += contract_first(raw, back_gate).reshape(QUARTERS, rows, width)


def gradient_share(tokens, ends, taps, weight, row, parts):
    runs, length, width = tokens.shape
    shape = (QUARTERS, weight.shape[0] // QUARTERS + PAD, width)
    counts = [part.shape[1] for part in parts]
    starts = [sum(counts[:i]) for i in range(len(counts))]
    return pl.pallas_call(
        functools.partial(gradient_kernel, starts),
        grid=(runs,),
        in_specs=[
            pl.BlockSpec((1, length, width), lambda r: (r, 0, 0)),
            pl.BlockSpec((1, 2, width), lambda r: (r, 0, 0)),
            pl.BlockSpec(taps.shape, lambda r: (0, 0)),
            pl.BlockSpec(weight.shape, lambda r: (0, 0)),
            pl.BlockSpec((1, length, length), lambda r: (r, 0, 0)),
        ]
        + [pl.BlockSpec(part.shape, lambda r: (0, 0, 0, 0)) for part in parts],
        out_specs=pl.BlockSpec(shape, lambda r: (0, 0, 0)),
        out_shape=jax.ShapeDtypeStruct(shape, F32),
        scratch_shapes=[pltpu.VMEM((width // LANES, length * runs, LANES), F32)],
        compiler_params=params(),
        cost_estimate=cost(
            2 * runs * length * width * (length + 2 * width),
            2 * runs * length * (length + 2 * width),
        ),
    )(tokens, ends, taps, weight, row, *parts)


def exchange(block):
    return lax.all_to_all(block, "ctx", split_axis=0, concat_axis=0, tiled=True)


def swapped(value, step, peers):
    return lax.ppermute(value, "ctx", [(i, i ^ step) for i in range(peers)])


def summed_quarter(share, peers):
    own = lax.axis_index("ctx") % QUARTERS
    quarter = lax.dynamic_index_in_dim(share, own, 0, keepdims=False)
    for step in range(1, QUARTERS):
        other = lax.dynamic_index_in_dim(share, own ^ step, 0, keepdims=False)
        quarter = quarter + swapped(other, step, peers)
    step = QUARTERS
    while step < peers:
        quarter = quarter + swapped(quarter, step, peers)
        step *= 2
    return quarter


def gathered(quarter, peers):
    own = lax.axis_index("ctx") % QUARTERS
    held = [quarter] + [swapped(quarter, step, peers) for step in range(1, QUARTERS)]
    for bit in (1, 2):
        odd = (own & bit) != 0
        held = [jnp.where(odd, held[i ^ bit], held[i]) for i in range(QUARTERS)]
    return held


def split(count, parts):
    return [count * part // sum(parts) for part in parts]


def local(tokens, conv_taps, gate_weight, row_factor, col_factor, cotangent):
    peers = lax.axis_size("ctx")
    width = tokens.shape[1]
    runs, length, _ = row_factor.shape
    offsets = col_factor.shape[0]
    rows = tokens.reshape(runs, length, width)

    back_got = []
    start = 0
    for count in split(offsets, BACK_PARTS):
        block = back_first_part(peers, col_factor, cotangent, start, count)
        if back_got:
            up = [(i, i + 1) for i in range(peers - 1)]
            down = [(i + 1, i) for i in range(peers - 1)]
            low = lax.ppermute(tokens[-1:], "ctx", up)
            high = lax.ppermute(tokens[:1], "ctx", down)
            block, low, high, back_got[0] = lax.optimization_barrier((block, low, high, back_got[0]))
        back_got.append(exchange(block))
        start += count

    before = jnp.concatenate([low, rows[:-1, -1]], axis=0)
    after = jnp.concatenate([rows[1:, 0], high], axis=0)
    ends = jnp.stack([before, after], axis=1).astype(F32)
    counts = split(offsets, FORWARD_PARTS)
    sent = list(first_parts(peers, rows, ends, conv_taps, gate_weight, row_factor, counts))
    sent[0], back_got[-1] = lax.optimization_barrier((sent[0], back_got[-1]))
    got = [exchange(sent[0])]

    share = gradient_share(rows, ends, conv_taps, gate_weight, row_factor, back_got)
    quarter = summed_quarter(share, peers)
    sent[1], got[0], quarter = lax.optimization_barrier((sent[1], got[0], quarter))
    got.append(exchange(sent[1]))
    held = gathered(quarter, peers)
    n_rows = quarter.shape[0] - PAD
    gate_grad = jnp.concatenate([part[:n_rows] for part in held], axis=0)
    conv_grad = jnp.concatenate([part[n_rows : n_rows + 1] for part in held[: conv_taps.shape[0]]], axis=0)

    mixed = mixed_part(col_factor, got[0], 0, None, VMEM_LIMIT // 4 * 3)
    rest, _ = lax.optimization_barrier((col_factor[counts[0] :], quarter))
    mixed = last_mixed_part(rest, got[1], counts[0], mixed)
    return (mixed, conv_grad, gate_grad)


def solution(mesh):
    placed = (
        P("ctx", "chan"),
        P(None, "chan"),
        P("chan", None),
        P("ctx", None, None),
        P("ctx", None, None),
        P("ctx", None, "chan"),
    )
    return jax.shard_map(
        local,
        mesh=mesh,
        in_specs=placed,
        out_specs=(P("ctx", None, "chan"), P(None, "chan"), P("chan", None)),
        check_vma=False,
    )
```

```python
import functools

import jax
import jax.numpy as jnp
from jax import lax
from jax.experimental import pallas as pl
from jax.experimental.pallas import tpu as pltpu
from jax.sharding import PartitionSpec as P

F32 = jnp.float32
BF16 = jnp.bfloat16
LANES = 128
GROUP = 4
QUARTERS = 4
PAD = 8
BACK_PARTS = (1, 3)
FORWARD_PARTS = (3, 1)
VMEM_LIMIT = 63 * 1024 * 1024 + 768 * 1024


def params():
    return pltpu.CompilerParams(vmem_limit_bytes=VMEM_LIMIT)


def cost(flops, moved):
    return pl.CostEstimate(flops=flops, bytes_accessed=moved, transcendentals=0)


def contract_first(lhs, rhs):
    return lax.dot_general(lhs, rhs, (((0,), (0,)), ((), ())), preferred_element_type=F32)


def copies(pairs, sems, at):
    return [pltpu.make_async_copy(source, target, sems.at[at + i]) for i, (source, target) in enumerate(pairs)]


def back_first_kernel(peers, group, first, col, cot, out, col_held, cot_held, out_held, in_sems, out_sems):
    offsets, _, width = cot_held.shape
    runs = out_held.shape[2]
    steps = [pl.ds(start, group) for start in range(0, offsets, group)]
    loads = [
        copies(
            [
                (col.at[pl.ds(first + i * group, group)], col_held.at[at]),
                (cot.at[pl.ds(first + i * group, group)], cot_held.at[at]),
            ],
            in_sems,
            2 * i,
        )
        for i, at in enumerate(steps)
    ]
    stores = [copies([(out_held.at[:, at], out.at[:, at])], out_sems, i) for i, at in enumerate(steps)]
    for load in loads:
        for copy in load:
            copy.start()
    for i, at in enumerate(steps):
        for copy in loads[i]:
            copy.wait()
        for d in range(i * group, (i + 1) * group):
            value = contract_first(col_held[d], cot_held[d]).astype(BF16)
            out_held[:, d] = value.reshape(peers, runs, width)
        stores[i][0].start()
    for store in stores:
        store[0].wait()


def back_first_part(peers, col, cot, start, count):
    _, order, runs_all = col.shape
    width = cot.shape[2]
    shape = (peers, count, runs_all // peers, width)
    group = GROUP if start else max(1, GROUP // 2)
    steps = count // group
    return pl.pallas_call(
        functools.partial(back_first_kernel, peers, group, start),
        in_specs=[pl.BlockSpec(memory_space=pl.ANY)] * 2,
        out_specs=pl.BlockSpec(memory_space=pl.ANY),
        out_shape=jax.ShapeDtypeStruct(shape, BF16),
        scratch_shapes=[
            pltpu.VMEM((count, order, runs_all), BF16),
            pltpu.VMEM((count, order, width), BF16),
            pltpu.VMEM(shape, BF16),
            pltpu.SemaphoreType.DMA((2 * steps,)),
            pltpu.SemaphoreType.DMA((steps,)),
        ],
        compiler_params=params(),
        cost_estimate=cost(
            2 * count * order * runs_all * width, 2 * count * (order * runs_all + 2 * order * width)
        ),
    )(col, cot)


def mixed_kernel(group, first, col, recv, *refs):
    out, col_held, recv_held, out_held, in_sems, out_sems = refs[-6:]
    peers, offsets, runs, width = recv_held.shape
    steps = [pl.ds(start, group) for start in range(0, offsets, group)]
    rows = [pl.ds(first + start, group) for start in range(0, offsets, group)]
    loads = [
        copies([(col.at[row], col_held.at[at]), (recv.at[:, at], recv_held.at[:, at])], in_sems, 2 * i)
        for i, (row, at) in enumerate(zip(rows, steps))
    ]
    stores = [
        copies([(out_held.at[at], out.at[row])], out_sems, i) for i, (row, at) in enumerate(zip(rows, steps))
    ]
    for load in loads:
        for copy in load:
            copy.start()
    for i in range(len(steps)):
        for copy in loads[i]:
            copy.wait()
        for d in range(i * group, (i + 1) * group):
            value = recv_held[:, d].reshape(peers * runs, width)
            out_held[d] = jnp.dot(col_held[d], value, preferred_element_type=F32).astype(BF16)
        stores[i][0].start()
    for store in stores:
        store[0].wait()


def mixed_part(col, recv, start, before, grant):
    offsets, order, runs_all = col.shape
    count, width = recv.shape[1], recv.shape[3]
    steps = count // GROUP
    operands = [col, recv] if before is None else [col, recv, before]
    return pl.pallas_call(
        functools.partial(mixed_kernel, GROUP, start),
        in_specs=[pl.BlockSpec(memory_space=pl.ANY)] * len(operands),
        out_specs=pl.BlockSpec(memory_space=pl.ANY),
        out_shape=jax.ShapeDtypeStruct((offsets, order, width), BF16),
        input_output_aliases={} if before is None else {2: 0},
        scratch_shapes=[
            pltpu.VMEM((count, order, runs_all), BF16),
            pltpu.VMEM(recv.shape, BF16),
            pltpu.VMEM((count, order, width), BF16),
            pltpu.SemaphoreType.DMA((2 * steps,)),
            pltpu.SemaphoreType.DMA((steps,)),
        ],
        compiler_params=pltpu.CompilerParams(vmem_limit_bytes=grant),
        cost_estimate=cost(
            2 * count * order * runs_all * width, 2 * count * (order * runs_all + 2 * order * width)
        ),
    )(*operands)


def last_mixed_kernel(group, first, col, recv, before, out, out_held, sems):
    peers, offsets, runs, width = recv.shape
    stores = []
    for start in range(0, offsets, group):
        for d in range(start, start + group):
            value = recv[:, d].reshape(peers * runs, width)
            out_held[d] = jnp.dot(col[d], value, preferred_element_type=F32).astype(BF16)
        pair = (out_held.at[pl.ds(start, group)], out.at[pl.ds(first + start, group)])
        stores += copies([pair], sems, len(stores))
        stores[-1].start()
    for store in stores:
        store.wait()


def last_mixed_part(col, recv, start, before):
    count, order, runs_all = col.shape
    width = recv.shape[3]
    steps = count // GROUP
    vmem = pl.BlockSpec(memory_space=pltpu.VMEM)
    return pl.pallas_call(
        functools.partial(last_mixed_kernel, GROUP, start),
        in_specs=[vmem, vmem, pl.BlockSpec(memory_space=pl.ANY)],
        out_specs=pl.BlockSpec(memory_space=pl.ANY),
        out_shape=jax.ShapeDtypeStruct(before.shape, BF16),
        input_output_aliases={2: 0},
        scratch_shapes=[pltpu.VMEM((count, order, width), BF16), pltpu.SemaphoreType.DMA((steps,))],
        compiler_params=pltpu.CompilerParams(vmem_limit_bytes=VMEM_LIMIT // 4),
        cost_estimate=cost(
            2 * count * order * runs_all * width, 2 * count * (order * runs_all + 2 * order * width)
        ),
    )(col, recv, before)


def shifted(tokens, before, after):
    count = tokens.shape[0]
    at = lax.broadcasted_iota(jnp.int32, tokens.shape, 0)
    low = jnp.where(at == 0, before, pltpu.roll(tokens, 1, 0))
    high = jnp.where(at == count - 1, after, pltpu.roll(tokens, count - 1, 0))
    return low, high


def conv_and_sig(tokens_ref, ends_ref, taps_ref, weight_ref):
    raw = tokens_ref[0]
    tokens = raw.astype(F32)
    low, high = shifted(tokens, ends_ref[0, 0:1], ends_ref[0, 1:2])
    conv = taps_ref[0:1] * low + taps_ref[1:2] * tokens + taps_ref[2:3] * high
    sig = jax.nn.sigmoid(jnp.dot(raw, weight_ref[...], preferred_element_type=F32))
    return raw, tokens, low, high, conv, sig


def first_kernel(peers, starts, tokens_ref, ends_ref, taps_ref, weight_ref, row_ref, *refs):
    outs, held = refs[:-1], refs[-1]
    run = pl.program_id(0)
    runs = pl.num_programs(0)
    count = tokens_ref.shape[1]
    n_runs = outs[0].shape[2]
    _, _, _, _, conv, sig = conv_and_sig(tokens_ref, ends_ref, taps_ref, weight_ref)
    gated = (conv * sig).astype(BF16)
    value = jnp.dot(row_ref[0], gated, preferred_element_type=F32)
    for lane in range(held.shape[0]):
        held[lane, pl.ds(run, count, stride=n_runs), :] = value[:, lane * LANES : (lane + 1) * LANES]

    @pl.when(run == runs - 1)
    def _():
        per_peer = count // peers
        for out, start in zip(outs, starts):
            rows = out.shape[1] * n_runs
            for peer in range(peers):
                at = (peer * per_peer + start) * n_runs
                for lane in range(held.shape[0]):
                    value = held[lane, pl.ds(at, rows), :].astype(BF16)
                    out[peer, :, :, lane * LANES : (lane + 1) * LANES] = value.reshape(out.shape[1], n_runs, LANES)


def first_parts(peers, tokens, ends, taps, weight, row, counts):
    runs, length, width = tokens.shape
    starts = [sum(counts[:i]) for i in range(len(counts))]
    return pl.pallas_call(
        functools.partial(first_kernel, peers, starts),
        grid=(runs,),
        in_specs=[
            pl.BlockSpec((1, length, width), lambda r: (r, 0, 0)),
            pl.BlockSpec((1, 2, width), lambda r: (r, 0, 0)),
            pl.BlockSpec(taps.shape, lambda r: (0, 0)),
            pl.BlockSpec(weight.shape, lambda r: (0, 0)),
            pl.BlockSpec((1, length, length), lambda r: (r, 0, 0)),
        ],
        out_specs=[pl.BlockSpec((peers, c, runs, width), lambda r: (0, 0, 0, 0)) for c in counts],
        out_shape=[jax.ShapeDtypeStruct((peers, c, runs, width), BF16) for c in counts],
        scratch_shapes=[pltpu.VMEM((width // LANES, length * runs, LANES), F32)],
        compiler_params=params(),
        cost_estimate=cost(
            2 * runs * length * width * (length + width), 2 * runs * length * (length + 2 * width)
        ),
    )(tokens, ends, taps, weight, row)


def gradient_kernel(starts, tokens_ref, ends_ref, taps_ref, weight_ref, row_ref, *refs):
    parts, (share_ref, held) = refs[:-2], refs[-2:]
    run = pl.program_id(0)
    count = tokens_ref.shape[1]
    peers, _, n_runs, width = parts[0].shape
    per_peer = count // peers
    rows = share_ref.shape[1] - PAD

    @pl.when(run == 0)
    def _():
        share_ref[...] = jnp.zeros_like(share_ref)
        for part, start in zip(parts, starts):
            got = part.shape[1] * n_runs
            for peer in range(peers):
                at = (peer * per_peer + start) * n_runs
                for lane in range(held.shape[0]):
                    value = part[peer, :, :, lane * LANES : (lane + 1) * LANES]
                    held[lane, pl.ds(at, got), :] = value.reshape(got, LANES).astype(F32)

    raw, tokens, low, high, conv, sig = conv_and_sig(tokens_ref, ends_ref, taps_ref, weight_ref)
    back_first = jnp.concatenate(
        [held[lane, pl.ds(run, count, stride=n_runs), :].astype(BF16) for lane in range(held.shape[0])], axis=1
    )
    back_conv = contract_first(row_ref[0], back_first) * sig
    for j, value in enumerate((low, tokens, high)):
        share_ref[j, rows : rows + 1] += jnp.sum(back_conv * value, axis=0, keepdims=True)
    back_gate = (back_conv * conv * (1.0 - sig)).astype(BF16)
    share_ref[:, :rows] += contract_first(raw, back_gate).reshape(QUARTERS, rows, width)


def gradient_share(tokens, ends, taps, weight, row, parts):
    runs, length, width = tokens.shape
    shape = (QUARTERS, weight.shape[0] // QUARTERS + PAD, width)
    counts = [part.shape[1] for part in parts]
    starts = [sum(counts[:i]) for i in range(len(counts))]
    return pl.pallas_call(
        functools.partial(gradient_kernel, starts),
        grid=(runs,),
        in_specs=[
            pl.BlockSpec((1, length, width), lambda r: (r, 0, 0)),
            pl.BlockSpec((1, 2, width), lambda r: (r, 0, 0)),
            pl.BlockSpec(taps.shape, lambda r: (0, 0)),
            pl.BlockSpec(weight.shape, lambda r: (0, 0)),
            pl.BlockSpec((1, length, length), lambda r: (r, 0, 0)),
        ]
        + [pl.BlockSpec(part.shape, lambda r: (0, 0, 0, 0)) for part in parts],
        out_specs=pl.BlockSpec(shape, lambda r: (0, 0, 0)),
        out_shape=jax.ShapeDtypeStruct(shape, F32),
        scratch_shapes=[pltpu.VMEM((width // LANES, length * runs, LANES), F32)],
        compiler_params=params(),
        cost_estimate=cost(
            2 * runs * length * width * (length + 2 * width),
            2 * runs * length * (length + 2 * width),
        ),
    )(tokens, ends, taps, weight, row, *parts)


def exchange(block):
    return lax.all_to_all(block, "ctx", split_axis=0, concat_axis=0, tiled=True)


def swapped(value, step, peers):
    return lax.ppermute(value, "ctx", [(i, i ^ step) for i in range(peers)])


def summed_quarter(share, peers):
    own = lax.axis_index("ctx") % QUARTERS
    quarter = lax.dynamic_index_in_dim(share, own, 0, keepdims=False)
    for step in range(1, QUARTERS):
        other = lax.dynamic_index_in_dim(share, own ^ step, 0, keepdims=False)
        quarter = quarter + swapped(other, step, peers)
    step = QUARTERS
    while step < peers:
        quarter = quarter + swapped(quarter, step, peers)
        step *= 2
    return quarter


def gathered(quarter, peers):
    own = lax.axis_index("ctx") % QUARTERS
    held = [quarter] + [swapped(quarter, step, peers) for step in range(1, QUARTERS)]
    for bit in (1, 2):
        odd = (own & bit) != 0
        held = [jnp.where(odd, held[i ^ bit], held[i]) for i in range(QUARTERS)]
    return held


def split(count, parts):
    return [count * part // sum(parts) for part in parts]


def local(tokens, conv_taps, gate_weight, row_factor, col_factor, cotangent):
    peers = lax.axis_size("ctx")
    width = tokens.shape[1]
    runs, length, _ = row_factor.shape
    offsets = col_factor.shape[0]
    rows = tokens.reshape(runs, length, width)

    back_got = []
    start = 0
    for count in split(offsets, BACK_PARTS):
        block = back_first_part(peers, col_factor, cotangent, start, count)
        if back_got:
            up = [(i, i + 1) for i in range(peers - 1)]
            down = [(i + 1, i) for i in range(peers - 1)]
            low = lax.ppermute(tokens[-1:], "ctx", up)
            high = lax.ppermute(tokens[:1], "ctx", down)
            block, low, high, back_got[0] = lax.optimization_barrier((block, low, high, back_got[0]))
        back_got.append(exchange(block))
        start += count

    before = jnp.concatenate([low, rows[:-1, -1]], axis=0)
    after = jnp.concatenate([rows[1:, 0], high], axis=0)
    ends = jnp.stack([before, after], axis=1).astype(F32)
    counts = split(offsets, FORWARD_PARTS)
    sent = list(first_parts(peers, rows, ends, conv_taps, gate_weight, row_factor, counts))
    sent[0], back_got[-1] = lax.optimization_barrier((sent[0], back_got[-1]))
    got = [exchange(sent[0])]

    share = gradient_share(rows, ends, conv_taps, gate_weight, row_factor, back_got)
    quarter = summed_quarter(share, peers)
    sent[1], got[0], quarter = lax.optimization_barrier((sent[1], got[0], quarter))
    got.append(exchange(sent[1]))
    held = gathered(quarter, peers)
    n_rows = quarter.shape[0] - PAD
    gate_grad = jnp.concatenate([part[:n_rows] for part in held], axis=0)
    conv_grad = jnp.concatenate([part[n_rows : n_rows + 1] for part in held[: conv_taps.shape[0]]], axis=0)

    mixed = mixed_part(col_factor, got[0], 0, None, VMEM_LIMIT // 4 * 3)
    rest, _ = lax.optimization_barrier((col_factor[counts[0] :], quarter))
    mixed = last_mixed_part(rest, got[1], counts[0], mixed)
    return (mixed, conv_grad, gate_grad)


def solution(mesh):
    placed = (
        P("ctx", "chan"),
        P(None, "chan"),
        P("chan", None),
        P("ctx", None, None),
        P("ctx", None, None),
        P("ctx", None, "chan"),
    )
    return jax.shard_map(
        local,
        mesh=mesh,
        in_specs=placed,
        out_specs=(P("ctx", None, "chan"), P(None, "chan"), P("chan", None)),
        check_vma=False,
    )
```

```python
import functools

import jax
import jax.numpy as jnp
from jax import lax
from jax.experimental import pallas as pl
from jax.experimental.pallas import tpu as pltpu
from jax.sharding import PartitionSpec as P

F32 = jnp.float32
BF16 = jnp.bfloat16
LANES = 128
GROUP = 4
QUARTERS = 4
PAD = 8
BACK_PARTS = (1, 3)
FORWARD_PARTS = (3, 1)
VMEM_LIMIT = 63 * 1024 * 1024 + 768 * 1024


def params():
    return pltpu.CompilerParams(vmem_limit_bytes=VMEM_LIMIT)


def cost(flops, moved):
    return pl.CostEstimate(flops=flops, bytes_accessed=moved, transcendentals=0)


def contract_first(lhs, rhs):
    return lax.dot_general(lhs, rhs, (((0,), (0,)), ((), ())), preferred_element_type=F32)


def copies(pairs, sems, at):
    return [pltpu.make_async_copy(source, target, sems.at[at + i]) for i, (source, target) in enumerate(pairs)]


def back_first_kernel(peers, group, first, col, cot, out, col_held, cot_held, out_held, in_sems, out_sems):
    offsets, _, width = cot_held.shape
    runs = out_held.shape[2]
    steps = [pl.ds(start, group) for start in range(0, offsets, group)]
    loads = [
        copies(
            [
                (col.at[pl.ds(first + i * group, group)], col_held.at[at]),
                (cot.at[pl.ds(first + i * group, group)], cot_held.at[at]),
            ],
            in_sems,
            2 * i,
        )
        for i, at in enumerate(steps)
    ]
    stores = [copies([(out_held.at[:, at], out.at[:, at])], out_sems, i) for i, at in enumerate(steps)]
    for load in loads:
        for copy in load:
            copy.start()
    for i, at in enumerate(steps):
        for copy in loads[i]:
            copy.wait()
        for d in range(i * group, (i + 1) * group):
            value = contract_first(col_held[d], cot_held[d]).astype(BF16)
            out_held[:, d] = value.reshape(peers, runs, width)
        stores[i][0].start()
    for store in stores:
        store[0].wait()


def back_first_part(peers, col, cot, start, count):
    _, order, runs_all = col.shape
    width = cot.shape[2]
    shape = (peers, count, runs_all // peers, width)
    group = GROUP if start else max(1, GROUP // 2)
    steps = count // group
    return pl.pallas_call(
        functools.partial(back_first_kernel, peers, group, start),
        in_specs=[pl.BlockSpec(memory_space=pl.ANY)] * 2,
        out_specs=pl.BlockSpec(memory_space=pl.ANY),
        out_shape=jax.ShapeDtypeStruct(shape, BF16),
        scratch_shapes=[
            pltpu.VMEM((count, order, runs_all), BF16),
            pltpu.VMEM((count, order, width), BF16),
            pltpu.VMEM(shape, BF16),
            pltpu.SemaphoreType.DMA((2 * steps,)),
            pltpu.SemaphoreType.DMA((steps,)),
        ],
        compiler_params=params(),
        cost_estimate=cost(
            2 * count * order * runs_all * width, 2 * count * (order * runs_all + 2 * order * width)
        ),
    )(col, cot)


def mixed_kernel(group, first, col, recv, *refs):
    out, col_held, recv_held, out_held, in_sems, out_sems = refs[-6:]
    peers, offsets, runs, width = recv_held.shape
    steps = [pl.ds(start, group) for start in range(0, offsets, group)]
    rows = [pl.ds(first + start, group) for start in range(0, offsets, group)]
    loads = [
        copies([(col.at[row], col_held.at[at]), (recv.at[:, at], recv_held.at[:, at])], in_sems, 2 * i)
        for i, (row, at) in enumerate(zip(rows, steps))
    ]
    stores = [
        copies([(out_held.at[at], out.at[row])], out_sems, i) for i, (row, at) in enumerate(zip(rows, steps))
    ]
    for load in loads:
        for copy in load:
            copy.start()
    for i in range(len(steps)):
        for copy in loads[i]:
            copy.wait()
        for d in range(i * group, (i + 1) * group):
            value = recv_held[:, d].reshape(peers * runs, width)
            out_held[d] = jnp.dot(col_held[d], value, preferred_element_type=F32).astype(BF16)
        stores[i][0].start()
    for store in stores:
        store[0].wait()


def mixed_part(col, recv, start, before, grant):
    offsets, order, runs_all = col.shape
    count, width = recv.shape[1], recv.shape[3]
    steps = count // GROUP
    operands = [col, recv] if before is None else [col, recv, before]
    return pl.pallas_call(
        functools.partial(mixed_kernel, GROUP, start),
        in_specs=[pl.BlockSpec(memory_space=pl.ANY)] * len(operands),
        out_specs=pl.BlockSpec(memory_space=pl.ANY),
        out_shape=jax.ShapeDtypeStruct((offsets, order, width), BF16),
        input_output_aliases={} if before is None else {2: 0},
        scratch_shapes=[
            pltpu.VMEM((count, order, runs_all), BF16),
            pltpu.VMEM(recv.shape, BF16),
            pltpu.VMEM((count, order, width), BF16),
            pltpu.SemaphoreType.DMA((2 * steps,)),
            pltpu.SemaphoreType.DMA((steps,)),
        ],
        compiler_params=pltpu.CompilerParams(vmem_limit_bytes=grant),
        cost_estimate=cost(
            2 * count * order * runs_all * width, 2 * count * (order * runs_all + 2 * order * width)
        ),
    )(*operands)


def last_mixed_kernel(group, first, col, recv, before, out, out_held, sems):
    peers, offsets, runs, width = recv.shape
    stores = []
    for start in range(0, offsets, group):
        for d in range(start, start + group):
            value = recv[:, d].reshape(peers * runs, width)
            out_held[d] = jnp.dot(col[d], value, preferred_element_type=F32).astype(BF16)
        pair = (out_held.at[pl.ds(start, group)], out.at[pl.ds(first + start, group)])
        stores += copies([pair], sems, len(stores))
        stores[-1].start()
    for store in stores:
        store.wait()


def last_mixed_part(col, recv, start, before):
    count, order, runs_all = col.shape
    width = recv.shape[3]
    steps = count // (GROUP // 2)
    vmem = pl.BlockSpec(memory_space=pltpu.VMEM)
    return pl.pallas_call(
        functools.partial(last_mixed_kernel, GROUP // 2, start),
        in_specs=[vmem, vmem, pl.BlockSpec(memory_space=pl.ANY)],
        out_specs=pl.BlockSpec(memory_space=pl.ANY),
        out_shape=jax.ShapeDtypeStruct(before.shape, BF16),
        input_output_aliases={2: 0},
        scratch_shapes=[pltpu.VMEM((count, order, width), BF16), pltpu.SemaphoreType.DMA((steps,))],
        compiler_params=pltpu.CompilerParams(vmem_limit_bytes=VMEM_LIMIT // 4),
        cost_estimate=cost(
            2 * count * order * runs_all * width, 2 * count * (order * runs_all + 2 * order * width)
        ),
    )(col, recv, before)


def shifted(tokens, before, after):
    count = tokens.shape[0]
    at = lax.broadcasted_iota(jnp.int32, tokens.shape, 0)
    low = jnp.where(at == 0, before, pltpu.roll(tokens, 1, 0))
    high = jnp.where(at == count - 1, after, pltpu.roll(tokens, count - 1, 0))
    return low, high


def conv_and_sig(tokens_ref, ends_ref, taps_ref, weight_ref):
    raw = tokens_ref[0]
    tokens = raw.astype(F32)
    low, high = shifted(tokens, ends_ref[0, 0:1], ends_ref[0, 1:2])
    conv = taps_ref[0:1] * low + taps_ref[1:2] * tokens + taps_ref[2:3] * high
    sig = jax.nn.sigmoid(jnp.dot(raw, weight_ref[...], preferred_element_type=F32))
    return raw, tokens, low, high, conv, sig


def first_kernel(peers, starts, tokens_ref, ends_ref, taps_ref, weight_ref, row_ref, *refs):
    outs, held = refs[:-1], refs[-1]
    run = pl.program_id(0)
    runs = pl.num_programs(0)
    count = tokens_ref.shape[1]
    n_runs = outs[0].shape[2]
    _, _, _, _, conv, sig = conv_and_sig(tokens_ref, ends_ref, taps_ref, weight_ref)
    gated = (conv * sig).astype(BF16)
    value = jnp.dot(row_ref[0], gated, preferred_element_type=F32)
    for lane in range(held.shape[0]):
        held[lane, pl.ds(run, count, stride=n_runs), :] = value[:, lane * LANES : (lane + 1) * LANES]

    @pl.when(run == runs - 1)
    def _():
        per_peer = count // peers
        for out, start in zip(outs, starts):
            rows = out.shape[1] * n_runs
            for peer in range(peers):
                at = (peer * per_peer + start) * n_runs
                for lane in range(held.shape[0]):
                    value = held[lane, pl.ds(at, rows), :].astype(BF16)
                    out[peer, :, :, lane * LANES : (lane + 1) * LANES] = value.reshape(out.shape[1], n_runs, LANES)


def first_parts(peers, tokens, ends, taps, weight, row, counts):
    runs, length, width = tokens.shape
    starts = [sum(counts[:i]) for i in range(len(counts))]
    return pl.pallas_call(
        functools.partial(first_kernel, peers, starts),
        grid=(runs,),
        in_specs=[
            pl.BlockSpec((1, length, width), lambda r: (r, 0, 0)),
            pl.BlockSpec((1, 2, width), lambda r: (r, 0, 0)),
            pl.BlockSpec(taps.shape, lambda r: (0, 0)),
            pl.BlockSpec(weight.shape, lambda r: (0, 0)),
            pl.BlockSpec((1, length, length), lambda r: (r, 0, 0)),
        ],
        out_specs=[pl.BlockSpec((peers, c, runs, width), lambda r: (0, 0, 0, 0)) for c in counts],
        out_shape=[jax.ShapeDtypeStruct((peers, c, runs, width), BF16) for c in counts],
        scratch_shapes=[pltpu.VMEM((width // LANES, length * runs, LANES), F32)],
        compiler_params=params(),
        cost_estimate=cost(
            2 * runs * length * width * (length + width), 2 * runs * length * (length + 2 * width)
        ),
    )(tokens, ends, taps, weight, row)


def gradient_kernel(starts, tokens_ref, ends_ref, taps_ref, weight_ref, row_ref, *refs):
    parts, (share_ref, held) = refs[:-2], refs[-2:]
    run = pl.program_id(0)
    count = tokens_ref.shape[1]
    peers, _, n_runs, width = parts[0].shape
    per_peer = count // peers
    rows = share_ref.shape[1] - PAD

    @pl.when(run == 0)
    def _():
        share_ref[...] = jnp.zeros_like(share_ref)
        for part, start in zip(parts, starts):
            got = part.shape[1] * n_runs
            for peer in range(peers):
                at = (peer * per_peer + start) * n_runs
                for lane in range(held.shape[0]):
                    value = part[peer, :, :, lane * LANES : (lane + 1) * LANES]
                    held[lane, pl.ds(at, got), :] = value.reshape(got, LANES).astype(F32)

    raw, tokens, low, high, conv, sig = conv_and_sig(tokens_ref, ends_ref, taps_ref, weight_ref)
    back_first = jnp.concatenate(
        [held[lane, pl.ds(run, count, stride=n_runs), :].astype(BF16) for lane in range(held.shape[0])], axis=1
    )
    back_conv = contract_first(row_ref[0], back_first) * sig
    for j, value in enumerate((low, tokens, high)):
        share_ref[j, rows : rows + 1] += jnp.sum(back_conv * value, axis=0, keepdims=True)
    back_gate = (back_conv * conv * (1.0 - sig)).astype(BF16)
    share_ref[:, :rows] += contract_first(raw, back_gate).reshape(QUARTERS, rows, width)


def gradient_share(tokens, ends, taps, weight, row, parts):
    runs, length, width = tokens.shape
    shape = (QUARTERS, weight.shape[0] // QUARTERS + PAD, width)
    counts = [part.shape[1] for part in parts]
    starts = [sum(counts[:i]) for i in range(len(counts))]
    return pl.pallas_call(
        functools.partial(gradient_kernel, starts),
        grid=(runs,),
        in_specs=[
            pl.BlockSpec((1, length, width), lambda r: (r, 0, 0)),
            pl.BlockSpec((1, 2, width), lambda r: (r, 0, 0)),
            pl.BlockSpec(taps.shape, lambda r: (0, 0)),
            pl.BlockSpec(weight.shape, lambda r: (0, 0)),
            pl.BlockSpec((1, length, length), lambda r: (r, 0, 0)),
        ]
        + [pl.BlockSpec(part.shape, lambda r: (0, 0, 0, 0)) for part in parts],
        out_specs=pl.BlockSpec(shape, lambda r: (0, 0, 0)),
        out_shape=jax.ShapeDtypeStruct(shape, F32),
        scratch_shapes=[pltpu.VMEM((width // LANES, length * runs, LANES), F32)],
        compiler_params=params(),
        cost_estimate=cost(
            2 * runs * length * width * (length + 2 * width),
            2 * runs * length * (length + 2 * width),
        ),
    )(tokens, ends, taps, weight, row, *parts)


def exchange(block):
    return lax.all_to_all(block, "ctx", split_axis=0, concat_axis=0, tiled=True)


def swapped(value, step, peers):
    return lax.ppermute(value, "ctx", [(i, i ^ step) for i in range(peers)])


def summed_quarter(share, peers):
    own = lax.axis_index("ctx") % QUARTERS
    quarter = lax.dynamic_index_in_dim(share, own, 0, keepdims=False)
    for step in range(1, QUARTERS):
        other = lax.dynamic_index_in_dim(share, own ^ step, 0, keepdims=False)
        quarter = quarter + swapped(other, step, peers)
    step = QUARTERS
    while step < peers:
        quarter = quarter + swapped(quarter, step, peers)
        step *= 2
    return quarter


def gathered(quarter, peers):
    own = lax.axis_index("ctx") % QUARTERS
    held = [quarter] + [swapped(quarter, step, peers) for step in range(1, QUARTERS)]
    for bit in (1, 2):
        odd = (own & bit) != 0
        held = [jnp.where(odd, held[i ^ bit], held[i]) for i in range(QUARTERS)]
    return held


def split(count, parts):
    return [count * part // sum(parts) for part in parts]


def local(tokens, conv_taps, gate_weight, row_factor, col_factor, cotangent):
    peers = lax.axis_size("ctx")
    width = tokens.shape[1]
    runs, length, _ = row_factor.shape
    offsets = col_factor.shape[0]
    rows = tokens.reshape(runs, length, width)

    back_got = []
    start = 0
    for count in split(offsets, BACK_PARTS):
        block = back_first_part(peers, col_factor, cotangent, start, count)
        if back_got:
            up = [(i, i + 1) for i in range(peers - 1)]
            down = [(i + 1, i) for i in range(peers - 1)]
            low = lax.ppermute(tokens[-1:], "ctx", up)
            high = lax.ppermute(tokens[:1], "ctx", down)
            block, low, high, back_got[0] = lax.optimization_barrier((block, low, high, back_got[0]))
        back_got.append(exchange(block))
        start += count

    before = jnp.concatenate([low, rows[:-1, -1]], axis=0)
    after = jnp.concatenate([rows[1:, 0], high], axis=0)
    ends = jnp.stack([before, after], axis=1).astype(F32)
    counts = split(offsets, FORWARD_PARTS)
    sent = list(first_parts(peers, rows, ends, conv_taps, gate_weight, row_factor, counts))
    sent[0], back_got[-1] = lax.optimization_barrier((sent[0], back_got[-1]))
    got = [exchange(sent[0])]

    share = gradient_share(rows, ends, conv_taps, gate_weight, row_factor, back_got)
    quarter = summed_quarter(share, peers)
    sent[1], got[0], quarter = lax.optimization_barrier((sent[1], got[0], quarter))
    got.append(exchange(sent[1]))
    held = gathered(quarter, peers)
    n_rows = quarter.shape[0] - PAD
    gate_grad = jnp.concatenate([part[:n_rows] for part in held], axis=0)
    conv_grad = jnp.concatenate([part[n_rows : n_rows + 1] for part in held[: conv_taps.shape[0]]], axis=0)

    mixed = mixed_part(col_factor, got[0], 0, None, VMEM_LIMIT // 4 * 3)
    rest, _ = lax.optimization_barrier((col_factor[counts[0] :], quarter))
    mixed = last_mixed_part(rest, got[1], counts[0], mixed)
    return (mixed, conv_grad, gate_grad)


def solution(mesh):
    placed = (
        P("ctx", "chan"),
        P(None, "chan"),
        P("chan", None),
        P("ctx", None, None),
        P("ctx", None, None),
        P("ctx", None, "chan"),
    )
    return jax.shard_map(
        local,
        mesh=mesh,
        in_specs=placed,
        out_specs=(P("ctx", None, "chan"), P(None, "chan"), P("chan", None)),
        check_vma=False,
    )
```
